768 devices in a mesh: region: 12 (over z), group: 64 (over y, x, core).
Axes of the slice: x: 4, y: 8, z: 12, core: 2. Of those that a mesh axis runs over, the one named last changes fastest.
Arguments:
- coeffs: float32 [1536, 24576], P('group', 'region'), may hold values from -6 to 6
- region_of: int32 [24576, 1], P('region'), may hold values from 0 to 11; in each aligned block of 2048 rows (0 to 2047, 2048 to 4095, ...) at most 512 rows name the same one
- block_pairs: int32 [12, 64, 2], P('region'), may hold values from 0 to 47, as said below
- block_owner: int32 [12, 64], P('region'), may hold values from 0 to 63, each once within a row
Outputs:
- corrected: float32 [1536, 24576], P('group', 'region')
- margin_blocks: float32 [12, 64, 128, 128], P('region', 'group')
The draws below stay inside these ranges and needn't reach their ends.
Inputs may be any that keep to these rules, and one draw needn't show every extreme that they name: `region_of`: among the 2048 functions of one index of region at most 512 name the same region, and that many do in every draw. `block_pairs`: for each region 64 distinct pairs (I, J) of its 48 blocks with I <= J; all 48 pairs (I, I) are among them. `block_owner`: each region's row names every position once; index g of group holds positions g * 1 to (g + 1) - 1.
All inputs are finite; a program needn't handle non-finite values.
Results may differ from the reference program's by a relative error of at most 0.0003.
Values sent between devices are 32-bit elements; how exact they have to be, the bound alone decides.
A program may use at most 32 MiB of HBM per device.

```python
import math
import jax
import jax.numpy as jnp
import numpy as np
from jax import lax

COEFFICIENT_SIZE = 1536
FB = 128
BPS = 4
FD = 2048
NFUNC = 24576
CAP = 512
NBLK = 48
REGION_SLOTS = 6144
KPAIRS = 64
N_REGION = 12


def draw_block_pairs(key, part):
    key = jax.random.fold_in(key, 11)
    upper_table = np.stack(np.triu_indices(NBLK, 1), axis=1).astype(np.int32)
    upper_pairs = jnp.asarray(upper_table)
    diagonal = jnp.stack([jnp.arange(NBLK, dtype=jnp.int32), jnp.arange(NBLK, dtype=jnp.int32)], axis=1)

    def one_region(region_key):
        pick_key, order_key = jax.random.split(region_key)
        picked = jax.random.permutation(pick_key, upper_table.shape[0])[:KPAIRS - NBLK]
        listing = jnp.concatenate([diagonal, upper_pairs[picked]], axis=0)
        return listing[jax.random.permutation(order_key, KPAIRS)]
    return jax.vmap(one_region)(jax.random.split(key, N_REGION)).astype(jnp.int32)


def shard_levels(rng, shape, pieces, smallest, high):
    gain, own = 1.0, jax.random.fold_in(rng, 6)
    for axis_at, parts in pieces:
        draws = jnp.exp(jax.random.uniform(jax.random.fold_in(own, axis_at), (parts,), jnp.float32, smallest / len(pieces), high / len(pieces)))
        gain = gain * jnp.repeat(draws, shape[axis_at] // parts).reshape([-1 if axis == axis_at else 1 for axis in range(len(shape))])
    return gain


def deal_out(stream_key, own, number, rows, count, top, limit, lean):
    sequence = jax.random.permutation(stream_key, count)
    packed, ordinary = portions_of(count, rows * top, limit, lean, True), portions_of(count, rows * top, limit, lean, False)
    places = jnp.arange(count)

    def named(tallies, offset_by):
        used = int((tallies > 0).sum())
        fixed = max(1, used // 4)
        passed = fixed + (places - fixed + offset_by * (used - fixed)) % max(1, count - fixed)
        return jnp.zeros((count,), jnp.int32).at[sequence[jnp.where(places < fixed, places, passed)]].set(jnp.asarray(tallies, jnp.int32))

    tallies = jnp.where(number % 4 == 0, named(packed, number // 4), named(ordinary, number - number // 4 - 1))
    mixed = jax.random.permutation(jax.random.fold_in(own, 3), count)
    giver, taker = mixed[0:count // 2 * 2:2], mixed[1:count // 2 * 2:2]
    slack = jnp.minimum(tallies[giver] - 1, limit - tallies[taker]) // 2
    slack = jnp.where((giver == sequence[0]) | (taker == sequence[0]) | (tallies[taker] == 0), 0, jnp.maximum(slack, 0))
    passed = jax.random.randint(jax.random.fold_in(own, 4), (count // 2,), 0, 1 << 20) % (slack + 1)
    tallies = tallies.at[giver].add(-passed).at[taker].add(passed)
    members = jnp.searchsorted(jnp.cumsum(tallies), jnp.arange(rows * top), side="right").astype(jnp.int32)
    table = members.reshape(top, rows).T
    table = table[jax.random.permutation(jax.random.fold_in(own, 1), rows)]
    offset_by = jax.random.randint(jax.random.fold_in(own, 2), (rows, 1), 0, top)
    return jnp.take_along_axis(table, (jnp.arange(top)[None, :] + offset_by) % top, axis=1)


def portions_of(count, total, bound, slope, full):
    loads = [(1 << 20) // math.isqrt(standing ** slope) + 1 for standing in range(1, count + 1)]
    largest = bound if full else min(bound, max(-(-total // count), total * loads[0] // sum(loads)))
    least = 1 if total - largest >= count - 1 else 0
    holding, rest = [largest] + [least] * (count - 1), total - largest - least * (count - 1)
    while rest > 0:
        movable = [i for i in range(1, count) if holding[i] < largest] or [i for i in range(1, count) if holding[i] < bound]
        mass, budget = sum([loads[i] for i in movable]), rest
        for i in movable:
            more = min(bound - holding[i], max(1, budget * loads[i] // mass), rest)
            holding[i] = holding[i] + more
            rest = rest - more
    return np.array(holding)


def bell_draw(key, dims, spread, bound, cuts=(), kind=jnp.bfloat16):
    factor_of = shard_levels(key, dims, cuts, -0.22, 0.18) if cuts else 1.0
    result = jax.random.normal(key, dims, jnp.float32) * spread * factor_of
    return jnp.minimum(jnp.maximum(result, -bound), bound).astype(kind)


def setup_inputs(seed: int = 0) -> dict:
    streams_of = jax.random.split(jax.random.key(seed), 5)
    coeffs = bell_draw(streams_of[0], (COEFFICIENT_SIZE, NFUNC), 1.0, 6.0, ((0, 64), (1, 12)), jnp.float32)
    region_of_keys = jax.random.split(jax.random.fold_in(streams_of[1], 1), NFUNC // FD)
    region_of_turns = jax.random.permutation(jax.random.fold_in(streams_of[1], 3), NFUNC // FD)
    region_of = jax.vmap(lambda own, number: deal_out(jax.random.fold_in(streams_of[1], 2), own, number, FD, N_REGION, 1, CAP, 2))(region_of_keys, region_of_turns).reshape((NFUNC, 1))
    block_pairs = draw_block_pairs(jax.random.fold_in(streams_of[4], 71), 0)
    block_owner = jax.vmap(lambda own: jax.random.permutation(own, KPAIRS))(jax.random.split(streams_of[3], N_REGION)).reshape((N_REGION, KPAIRS)).astype(jnp.int32)
    return dict(coeffs=coeffs, region_of=region_of, block_pairs=block_pairs, block_owner=block_owner)


def slot_index(target, region_count, step_offset):
    onehot = (target[:, None] == jnp.arange(region_count, dtype=jnp.int32)[None, :]).astype(jnp.int32)
    rank_in = jnp.sum((jnp.cumsum(onehot, axis=0) - onehot) * onehot, axis=1)
    return (target * step_offset + rank_in).astype(jnp.int32)


def margin_of(regional, pair_list):
    left_cols = regional[:, pair_list[:, 0]]
    right_cols = regional[:, pair_list[:, 1]]
    return jnp.einsum('ckf,ckg->kfg', left_cols, right_cols, precision=lax.Precision.HIGHEST)


def change_of(regional, pair_list, blocks):
    left_idx = pair_list[:, 0]
    right_idx = pair_list[:, 1]
    on_diag = (left_idx == right_idx).astype(jnp.float32)
    identity = jnp.eye(blocks.shape[1], dtype=jnp.float32)
    shifted = blocks - identity[None] * on_diag[:, None, None]
    toward_leftward = jnp.einsum('ckg,kfg->ckf', regional[:, right_idx], shifted, precision=lax.Precision.HIGHEST)
    to_right = jnp.einsum('ckf,kfg->ckg', regional[:, left_idx], shifted, precision=lax.Precision.HIGHEST)
    to_right = to_right * (1.0 - on_diag)[None, :, None]
    block_count = regional.shape[1]
    numbers = jnp.arange(block_count, dtype=jnp.int32)[None, :]
    onehot_leftward = (left_idx[:, None] == numbers).astype(jnp.float32)
    hot_right = (right_idx[:, None] == numbers).astype(jnp.float32)
    leading_portion = jnp.einsum('atw,td->adw', toward_leftward, onehot_leftward, precision=lax.Precision.HIGHEST)
    second_part = jnp.einsum('ckg,kb->cbg', to_right, hot_right, precision=lax.Precision.HIGHEST)
    return leading_portion + second_part


def place_row(entry_value_list, function_slot_row):
    return jnp.zeros((COEFFICIENT_SIZE, REGION_SLOTS), entry_value_list.dtype).at[:, function_slot_row].set(entry_value_list)


def pick_row(entry_value_list, function_slot_row):
    return entry_value_list[:, function_slot_row]


def reference(coeffs, region_of, block_pairs, block_owner):
    step_offset = BPS * FB
    per_source = coeffs.reshape(COEFFICIENT_SIZE, N_REGION, FD).transpose(1, 0, 2)
    targets = region_of[:, 0].reshape(N_REGION, FD)
    slot_table = jax.vmap(lambda target: slot_index(target, N_REGION, step_offset))(targets)
    placed = jax.vmap(place_row)(per_source, slot_table)
    regional_all = placed.reshape(N_REGION, COEFFICIENT_SIZE, N_REGION, step_offset).transpose(2, 1, 0, 3).reshape(N_REGION, COEFFICIENT_SIZE, NBLK, FB)

    def per_region(inputs):
        regional, pair_list, owners = inputs
        blocks = margin_of(regional, pair_list) / COEFFICIENT_SIZE
        by_owner = jnp.zeros((KPAIRS,), jnp.int32).at[owners].set(jnp.arange(KPAIRS, dtype=jnp.int32))
        updated = regional - 0.5 * change_of(regional, pair_list, blocks)
        return updated, blocks[by_owner]

    refreshed_everything, owned_all = lax.map(per_region, (regional_all, block_pairs, block_owner))
    handed_result = refreshed_everything.reshape(N_REGION, COEFFICIENT_SIZE, N_REGION, step_offset).transpose(2, 1, 0, 3).reshape(N_REGION, COEFFICIENT_SIZE, REGION_SLOTS)
    picked = jax.vmap(pick_row)(handed_result, slot_table)
    corrected = picked.transpose(1, 0, 2).reshape(COEFFICIENT_SIZE, N_REGION * FD)
    return corrected, owned_all
```

```python
import functools

import jax
import jax.numpy as jnp
from jax import lax
from jax.experimental import pallas as pl
from jax.experimental.pallas import tpu as pltpu
from jax.sharding import PartitionSpec as P

COEFFICIENT_SIZE = 1536
FB = 128
BPS = 4
FD = 2048
NR = 12
NG = 64
NBLK = NR * BPS
NQ = NG // 4
ROWS = 24
NC = ROWS // 8
NT = 2 * NQ
PACKED = 28
MESH = pl.DeviceIdType.MESH
HIGHEST = lax.Precision.HIGHEST

T_UNIT = 0
T_PERM = T_UNIT + NT
T_SAME = T_PERM + NT
T_LAST = T_SAME + NT
T_IDX = T_LAST + NBLK
T_INV = T_IDX + NT
T_POS = T_INV + NBLK
T_END = T_POS + NG


def slot_index(target):
    onehot = (target[:, None] == jnp.arange(NR, dtype=jnp.int32)[None, :]).astype(jnp.int32)
    rank = jnp.sum((jnp.cumsum(onehot, axis=0) - onehot) * onehot, axis=1)
    return rank, jnp.sum(onehot, axis=0)


def pair_tables(pairs, owners):
    left, right = pairs[:, 0], pairs[:, 1]
    off = left != right
    number = jnp.arange(NG, dtype=jnp.int32)
    off_rank = jnp.sum((off[None, :] & (number[None, :] < number[:, None])).astype(jnp.int32), axis=1)
    pick = (off_rank[None, :] == jnp.arange(NQ, dtype=jnp.int32)[:, None]) & off[None, :]
    unit = jnp.stack(
        [jnp.sum(jnp.where(pick, left[None, :], 0), axis=1), jnp.sum(jnp.where(pick, right[None, :], 0), axis=1)],
        axis=1,
    ).reshape(NT)
    u = jnp.arange(NT, dtype=jnp.int32)
    key = unit * NT + u
    rank = jnp.sum((key[None, :] < key[:, None]).astype(jnp.int32), axis=1)
    at = rank[None, :] == u[:, None]
    perm = jnp.sum(jnp.where(at, u[None, :], 0), axis=1)
    ordered = jnp.sum(jnp.where(at, unit[None, :], 0), axis=1)
    same = jnp.concatenate([jnp.zeros((1,), jnp.int32), (ordered[1:] == ordered[:-1]).astype(jnp.int32)])
    b = jnp.arange(NBLK, dtype=jnp.int32)
    last = jnp.max(jnp.where(ordered[None, :] == b[:, None], u[None, :], -1), axis=1)
    last = jnp.where(last < 0, NT, last)
    piece = jnp.where(off, NBLK + off_rank, left)
    pos = jnp.sum(jnp.where(owners[None, :] == number[:, None], piece[None, :], 0), axis=1)
    return unit, perm, same, last, pos


def kernel(
    tab, x_ref, hi_ref, hip_ref, lo_ref, out_ref, margin_ref,
    oh_lo, masked, zout, zin, gdo, gdi, goo, goi, qd, qo, rdo, rdi, roo, roi, seg, zro, zri,
    mdo, mdi, mzo, mko, mall, mfo, mfi, upd, picked,
    ss, sr_z, sr_gd, sr_go, sr_qd, sr_qo, sr_rd, sr_ro, sr_zr, sr_md, sr_mz, sr_mo, sr_mf,
):
    r = lax.axis_index("region")
    g = lax.axis_index("group")
    me = lax.div(g, 4)
    h = lax.rem(g, 4)

    def z_peer(k):
        return lax.rem(r + k, NR)

    def c_peer(k):
        return lax.rem(me + k, NQ)

    def q_peer(k):
        return lax.rem(h + k, 4)

    barrier = pltpu.get_barrier_semaphore()

    def greet_z(k, _):
        pl.semaphore_signal(barrier, inc=1, device_id=(z_peer(k), g), device_id_type=MESH)
        return 0

    def greet_c(k, _):
        pl.semaphore_signal(barrier, inc=1, device_id=(r, c_peer(k) * 4 + h), device_id_type=MESH)
        return 0

    def greet_q(k, _):
        pl.semaphore_signal(barrier, inc=1, device_id=(r, me * 4 + q_peer(k)), device_id_type=MESH)
        return 0

    lax.fori_loop(1, NR, greet_z, 0)
    lax.fori_loop(1, NQ, greet_c, 0)
    lax.fori_loop(1, 4, greet_q, 0)

    def z_send(src, dst, sem_r, sem_s):
        def go(i, _):
            k = NR // 2 + lax.div(i + 1, 2) * (1 - 2 * lax.rem(i, 2))
            d = z_peer(k)
            pltpu.make_async_remote_copy(
                src_ref=src.at[pl.ds(d * BPS, BPS)], dst_ref=dst.at[pl.ds(r * BPS, BPS)],
                send_sem=sem_s, recv_sem=sem_r, device_id=(d, g), device_id_type=MESH,
            ).start()
            return 0

        lax.fori_loop(0, NR - 1, go, 0)

    def z_wait(src, dst, sem_r, sem_s):
        n = (NR - 1) * BPS
        c = pltpu.make_async_remote_copy(
            src_ref=src.at[pl.ds(0, n)], dst_ref=dst.at[pl.ds(0, n)],
            send_sem=sem_s, recv_sem=sem_r, device_id=(z_peer(1), g), device_id_type=MESH,
        )
        return c

    def c_send(src, dst, sem_r, sem_s, base=0):
        def go(k, _):
            m = c_peer(k)
            pltpu.make_async_remote_copy(
                src_ref=src.at[m], dst_ref=dst.at[base + me],
                send_sem=sem_s, recv_sem=sem_r, device_id=(r, m * 4 + h), device_id_type=MESH,
            ).start()
            return 0

        lax.fori_loop(1, NQ, go, 0)

    def c_wait(src, dst, sem_r, sem_s):
        return pltpu.make_async_remote_copy(
            src_ref=src.at[pl.ds(0, NQ - 1)], dst_ref=dst.at[pl.ds(0, NQ - 1)],
            send_sem=sem_s, recv_sem=sem_r, device_id=(r, c_peer(1) * 4 + h), device_id_type=MESH,
        )

    def q_send(buf, sem_r, sem_s):
        def go(k, _):
            o = q_peer(k)
            pltpu.make_async_remote_copy(
                src_ref=buf.at[h], dst_ref=buf.at[h],
                send_sem=sem_s, recv_sem=sem_r, device_id=(r, me * 4 + o), device_id_type=MESH,
            ).start()
            return 0

        lax.fori_loop(1, 4, go, 0)

    def q_wait(buf, sem_r, sem_s):
        return pltpu.make_async_remote_copy(
            src_ref=buf.at[pl.ds(0, 3)], dst_ref=buf.at[pl.ds(0, 3)],
            send_sem=sem_s, recv_sem=sem_r, device_id=(r, me * 4 + q_peer(1)), device_id_type=MESH,
        )

    zero = jnp.zeros((8, FB), jnp.float32)

    oh_lo[...] = jnp.where(
        lax.broadcasted_iota(jnp.int32, (FB, FD), 0) == lo_ref[...], 1.0, 0.0
    ).astype(jnp.bfloat16)
    hi = hi_ref[...]
    for c in range(NC):
        x = x_ref[pl.ds(8 * c, 8), :]
        big = x.astype(jnp.bfloat16)
        small = (x - big.astype(jnp.float32)).astype(jnp.bfloat16)
        both = jnp.concatenate([big, small], axis=0)
        for b in range(NBLK):
            keep = jnp.where(hi == b, 1.0, 0.0).astype(jnp.bfloat16)
            masked[pl.ds(16 * b, 16), :] = both * keep
        placed = lax.dot_general(
            masked[...], oh_lo[...], (((1,), (1,)), ((), ())), preferred_element_type=jnp.float32
        ).reshape(NBLK, 16, FB)
        zout[c][pl.ds(0, NBLK)] = placed[:, :8] + placed[:, 8:]
        zout[c][NBLK] = zero
        if c == 0:
            pl.semaphore_wait(barrier, (NR - 1) + (NQ - 1) + 3)
        z_send(zout[c], zin[c], sr_z.at[c], ss.at[12 + c])
        zin[c][pl.ds(r * BPS, BPS)] = zout[c][pl.ds(r * BPS, BPS)]

    for t in range(NT):
        for c in range(NC):
            gdo[t // 2, t % 2, c] = zout[c][tab[T_IDX + t]]
    c_send(gdo, gdi, sr_gd, ss.at[1])
    gdi[me] = gdo[me]
    c_wait(gdo, gdi, sr_gd, ss.at[1]).wait_recv()

    def block_of(ref, u):
        return ref[:, u].reshape(NQ * NC * 8, FB)

    def gram(a, b):
        return lax.dot_general(a, b, (((0,), (0,)), ((), ())), precision=HIGHEST, preferred_element_type=jnp.float32)

    for u in range(2):
        xu = block_of(gdi, u)
        qd[h, u] = gram(xu, xu)
    q_send(qd, sr_qd, ss.at[2])

    for c in range(NC):
        z_wait(zout[c], zin[c], sr_z.at[c], ss.at[12 + c]).wait_recv()
        for k in range(NQ):
            for u in range(2):
                goo[c][k, u] = zin[c][tab[T_UNIT + 2 * k + u]]
        c_send(goo[c], goi[c], sr_go.at[c], ss.at[15 + c])
        goi[c][me] = goo[c][me]

    q_wait(qd, sr_qd, ss.at[2]).wait_recv()
    eye = jnp.where(
        lax.broadcasted_iota(jnp.int32, (FB, FB), 0) == lax.broadcasted_iota(jnp.int32, (FB, FB), 1), 1.0, 0.0
    )
    for u in range(2):
        m = (qd[0, u] + qd[1, u] + qd[2, u] + qd[3, u]) * (1.0 / COEFFICIENT_SIZE)
        mdo[:, u] = m.reshape(NQ, 8, FB)
        change = jnp.dot(block_of(gdi, u), m - eye, precision=HIGHEST, preferred_element_type=jnp.float32)
        rdo[:, u] = change.reshape(NQ, NC, 8, FB)
    c_send(mdo, mdi, sr_md, ss.at[4])
    mdi[me] = mdo[me]

    for c in range(NC):
        c_wait(goo[c], goi[c], sr_go.at[c], ss.at[15 + c]).wait_recv()
    left = jnp.concatenate([goi[c][:, 0].reshape(NQ * 8, FB) for c in range(NC)], axis=0)
    right = jnp.concatenate([goi[c][:, 1].reshape(NQ * 8, FB) for c in range(NC)], axis=0)
    qo[h] = gram(left, right)
    q_send(qo, sr_qo, ss.at[5])

    c_wait(mdo, mdi, sr_md, ss.at[4]).wait_recv()
    for b in range(NBLK):
        t = tab[T_INV + b]
        mzo[b] = mdi[lax.div(t, 2), lax.rem(t, 2)]
    z_send(mzo, mall, sr_mz, ss.at[6])
    mall[pl.ds(r * BPS, BPS)] = mzo[pl.ds(r * BPS, BPS)]

    q_wait(qo, sr_qo, ss.at[5]).wait_recv()
    m = (qo[0] + qo[1] + qo[2] + qo[3]) * (1.0 / COEFFICIENT_SIZE)
    mko[...] = m.reshape(NQ, 8, FB)
    to_left = lax.dot_general(
        right, m, (((1,), (1,)), ((), ())), precision=HIGHEST, preferred_element_type=jnp.float32
    ).reshape(NC, NQ, 8, FB)
    to_right = jnp.dot(left, m, precision=HIGHEST, preferred_element_type=jnp.float32).reshape(NC, NQ, 8, FB)
    for c in range(NC):
        roo[c][:, 0] = to_left[c]
        roo[c][:, 1] = to_right[c]
        c_send(roo[c], roi[c], sr_ro.at[c], ss.at[18 + c])
        roi[c][me] = roo[c][me]

    c_send(mko, mall, sr_mo, ss.at[8], base=NBLK)
    mall[NBLK + me] = mko[me]
    c_send(rdo, rdi, sr_rd, ss.at[9])
    rdi[me] = rdo[me]

    seg[NT] = zero
    for c in range(NC):
        c_wait(roo[c], roi[c], sr_ro.at[c], ss.at[18 + c]).wait_recv()
        total = zero
        for i in range(NT):
            p = tab[T_PERM + i]
            total = roi[c][lax.div(p, 2), lax.rem(p, 2)] + total * tab[T_SAME + i].astype(jnp.float32)
            seg[i] = total
        for b in range(NBLK):
            zro[c][b] = seg[tab[T_LAST + b]]
        z_send(zro[c], zri[c], sr_zr.at[c], ss.at[21 + c])
        zri[c][pl.ds(r * BPS, BPS)] = zro[c][pl.ds(r * BPS, BPS)]
        zri[c][NBLK] = zero

    z_wait(mzo, mall, sr_mz, ss.at[6]).wait_recv()
    c_wait(mko, mall, sr_mo, ss.at[8]).wait_recv()
    for i in range(NQ):
        mfo[i] = mall[tab[T_POS + 4 * i + h]]
    c_send(mfo, mfi, sr_mf, ss.at[11])
    mfi[me] = mfo[me]

    c_wait(rdo, rdi, sr_rd, ss.at[9]).wait_recv()
    hip = hip_ref[...]
    for c in range(NC):
        z_wait(zro[c], zri[c], sr_zr.at[c], ss.at[21 + c]).wait_recv()
        for t in range(PACKED):
            u = gdo[t // 2, t % 2, c] - 0.5 * (rdi[t // 2, t % 2, c] + zri[c][tab[T_IDX + t]])
            big = u.astype(jnp.bfloat16)
            small = (u - big.astype(jnp.float32)).astype(jnp.bfloat16)
            upd[pl.ds(16 * t, 16), :] = jnp.concatenate([big, small], axis=0)
        picked[...] = jnp.dot(upd[...], oh_lo[...], preferred_element_type=jnp.float32)
        total = jnp.zeros((8, FD), jnp.float32)
        for t in range(PACKED):
            both = picked[pl.ds(16 * t, 8), :] + picked[pl.ds(16 * t + 8, 8), :]
            total = total + jnp.where(hip == t, both, 0.0)
        out_ref[pl.ds(8 * c, 8), :] = total

    c_wait(mfo, mfi, sr_mf, ss.at[11]).wait_recv()
    margin_ref[...] = mfi[...].reshape(FB, FB)

    for c in range(NC):
        z_wait(zout[c], zin[c], sr_z.at[c], ss.at[12 + c]).wait_send()
        c_wait(goo[c], goi[c], sr_go.at[c], ss.at[15 + c]).wait_send()
        c_wait(roo[c], roi[c], sr_ro.at[c], ss.at[18 + c]).wait_send()
        z_wait(zro[c], zri[c], sr_zr.at[c], ss.at[21 + c]).wait_send()
    c_wait(gdo, gdi, sr_gd, ss.at[1]).wait_send()
    q_wait(qd, sr_qd, ss.at[2]).wait_send()
    c_wait(mdo, mdi, sr_md, ss.at[4]).wait_send()
    q_wait(qo, sr_qo, ss.at[5]).wait_send()
    z_wait(mzo, mall, sr_mz, ss.at[6]).wait_send()
    c_wait(mko, mall, sr_mo, ss.at[8]).wait_send()
    c_wait(rdo, rdi, sr_rd, ss.at[9]).wait_send()
    c_wait(mfo, mfi, sr_mf, ss.at[11]).wait_send()


def body(coeffs, region_of, block_pairs, block_owner):
    target = region_of[:, 0]
    rank, count = slot_index(target)
    blocks = (count + FB - 1) // FB
    d = jnp.arange(NR, dtype=jnp.int32)
    start = jnp.sum(jnp.where(d[None, :] < d[:, None], blocks[None, :], 0), axis=1)
    b = jnp.arange(NBLK, dtype=jnp.int32)
    inv = jnp.where((b % BPS)[None, :].reshape(NR, BPS) < blocks[:, None], start[:, None] + (b % BPS).reshape(NR, BPS), NT - 1)
    inv = inv.reshape(NBLK)
    t = jnp.arange(NT, dtype=jnp.int32)
    idx = jnp.min(jnp.where((inv[None, :] == t[:, None]) & (t[:, None] < NT - 1), b[None, :], NBLK), axis=1)
    unit, perm, same, last, pos = pair_tables(block_pairs[0], block_owner[0])
    tab = jnp.concatenate([unit, perm, same, last, idx, inv, pos]).astype(jnp.int32)
    hi = target * BPS + rank // FB
    hip = jnp.sum(jnp.where(target[:, None] == d[None, :], start[None, :], 0), axis=1) + rank // FB
    lo = rank % FB

    f32, bf16 = jnp.float32, jnp.bfloat16
    v = pltpu.VMEM
    tile = (8, FB)
    dma = pltpu.SemaphoreType.DMA
    vm = pl.BlockSpec(memory_space=pltpu.VMEM)
    z = [v((NBLK + 1, *tile), f32) for _ in range(NC)]
    pr = [v((NQ, 2, *tile), f32) for _ in range(NC)]
    un = v((NQ, 2, NC, *tile), f32)
    corrected, margin = pl.pallas_call(
        kernel,
        out_shape=(jax.ShapeDtypeStruct((ROWS, FD), f32), jax.ShapeDtypeStruct((FB, FB), f32)),
        in_specs=[pl.BlockSpec(memory_space=pltpu.SMEM), vm, vm, vm, vm],
        out_specs=(vm, vm),
        scratch_shapes=[
            v((FB, FD), bf16), v((NBLK * 16, FD), bf16), z, z, un, un, pr, pr,
            v((4, 2, FB, FB), f32), v((4, FB, FB), f32), un, un, pr, pr, v((NT + 1, *tile), f32), z, z,
            v((NQ, 2, *tile), f32), v((NQ, 2, *tile), f32), v((NBLK, *tile), f32), v((NQ, *tile), f32),
            v((NG, *tile), f32), v((NQ, *tile), f32), v((NQ, *tile), f32),
            v((PACKED * 16, FB), bf16), v((PACKED * 16, FD), f32),
            dma((24,)), dma((NC,)), dma, dma((NC,)), dma, dma, dma, dma((NC,)), dma((NC,)), dma, dma, dma, dma,
        ],
        compiler_params=pltpu.CompilerParams(collective_id=0, has_side_effects=True, vmem_limit_bytes=56 * 2**20),
    )(tab, coeffs, hi[None, :], hip[None, :], lo[None, :])
    return corrected, margin[None, None]


def solution(mesh):
    placed = (P("group", "region"), P("region", None), P("region", None, None), P("region", None))
    return jax.shard_map(
        body,
        mesh=mesh,
        in_specs=placed,
        out_specs=(P("group", "region"), P("region", "group", None, None)),
        check_vma=False,
    )
```

```python
import functools

import jax
import jax.numpy as jnp
from jax import lax
from jax.experimental import pallas as pl
from jax.experimental.pallas import tpu as pltpu
from jax.sharding import PartitionSpec as P

COEFFICIENT_SIZE = 1536
FB = 128
BPS = 4
FD = 2048
NR = 12
NG = 64
NBLK = NR * BPS
NQ = NG // 4
ROWS = 24
NC = ROWS // 8
NT = 2 * NQ
PACKED = 28
MESH = pl.DeviceIdType.MESH
HIGHEST = lax.Precision.HIGHEST

T_UNIT, T_PERM, T_SAME, T_LAST, T_POS, T_IDX, T_INV = range(7)


def iota(shape, axis):
    return lax.broadcasted_iota(jnp.int32, shape, axis)


def column(row, n):
    spread = jnp.where(iota((n, FB), 0) == iota((n, FB), 1), row, 0)
    return jnp.sum(spread.astype(jnp.float32), axis=1, keepdims=True).astype(jnp.int32)


def pair_rows(left, right, owner_row):
    p, lane = iota((NG, FB), 0), iota((NG, FB), 1)
    off = (left != right).astype(jnp.int32)
    off_row = jnp.sum(jnp.where(p == lane, off, 0), axis=0, keepdims=True)
    before = jnp.where(lane < p, off_row, 0)
    off_rank = jnp.sum(before.astype(jnp.float32), axis=1, keepdims=True).astype(jnp.int32)
    hit = (lane < NT) & (off == 1) & (off_rank == lane % NQ)
    unit = jnp.sum(jnp.where(hit, jnp.where(lane < NQ, left, right), 0), axis=0, keepdims=True)
    u, r = iota((NT, FB), 0), iota((NT, FB), 1)
    dest = column(unit, NT)
    key_row = unit * NT + iota((1, FB), 1)
    key = dest * NT + iota((NT, 1), 0)
    smaller = jnp.where((r < NT) & (key_row < key), 1.0, 0.0)
    rank = jnp.sum(smaller, axis=1, keepdims=True).astype(jnp.int32)
    perm = jnp.sum(jnp.where(rank == r, u, 0), axis=0, keepdims=True)
    here = jnp.sum(jnp.where(rank == r, dest, 0), axis=0, keepdims=True)
    previous = jnp.sum(jnp.where(rank == r - 1, dest, 0), axis=0, keepdims=True)
    same = jnp.where((here == previous) & (iota((1, FB), 1) > 0), 1, 0)
    last = jnp.max(jnp.where(dest == r, rank, -1), axis=0, keepdims=True)
    last = jnp.where(last < 0, NT, last)
    piece = jnp.where(off == 1, NBLK + off_rank, left)
    pos = jnp.sum(jnp.where(column(owner_row, NG) == lane, piece, 0), axis=0, keepdims=True)
    return [unit, perm, same, last, pos]


def block_rows(start, blocks):
    d, t = iota((16, FB), 0), iota((16, FB), 1)
    inside = (t >= start) & (t < start + blocks)
    idx = jnp.sum(jnp.where(inside, d * BPS + t - start + 1, 0), axis=0, keepdims=True) - 1
    idx = jnp.where(idx < 0, NBLK, idx)
    mine = (t // BPS == d) & (t % BPS < blocks)
    inv = jnp.sum(jnp.where(mine, start + t % BPS + 1, 0), axis=0, keepdims=True) - 1
    inv = jnp.where(inv < 0, NT - 1, inv)
    return [idx, inv]


def kernel(
    x_ref, target_ref, pairs_ref, owner_ref, out_ref, margin_ref,
    tabv, tab, hip_ref, tab_sem, oh_lo, masked, zout, zin, gdo, gdi, goo, goi, qd, qo, rdo, rdi, roo, roi, seg, zro, zri,
    mdo, mdi, mzo, mko, mall, mfo, mfi, upd, picked,
    ss, sr_z, sr_gd, sr_go, sr_qd, sr_qo, sr_rd, sr_ro, sr_zr, sr_md, sr_mz, sr_mo, sr_mf,
):
    r = lax.axis_index("region")
    g = lax.axis_index("group")
    me = lax.div(g, 4)
    h = lax.rem(g, 4)

    def z_peer(k):
        return lax.rem(r + k, NR)

    def c_peer(k):
        return lax.rem(me + k, NQ)

    def q_peer(k):
        return lax.rem(h + k, 4)

    barrier = pltpu.get_barrier_semaphore()

    def greet_z(k, _):
        pl.semaphore_signal(barrier, inc=1, device_id=(z_peer(k), g), device_id_type=MESH)
        return 0

    def greet_c(k, _):
        pl.semaphore_signal(barrier, inc=1, device_id=(r, c_peer(k) * 4 + h), device_id_type=MESH)
        return 0

    def greet_q(k, _):
        pl.semaphore_signal(barrier, inc=1, device_id=(r, me * 4 + q_peer(k)), device_id_type=MESH)
        return 0

    lax.fori_loop(1, NR, greet_z, 0)
    lax.fori_loop(1, NQ, greet_c, 0)
    lax.fori_loop(1, 4, greet_q, 0)

    def z_send(src, dst, sem_r, sem_s):
        def go(i, _):
            k = NR // 2 + lax.div(i + 1, 2) * (1 - 2 * lax.rem(i, 2))
            d = z_peer(k)
            pltpu.make_async_remote_copy(
                src_ref=src.at[pl.ds(d * BPS, BPS)], dst_ref=dst.at[pl.ds(r * BPS, BPS)],
                send_sem=sem_s, recv_sem=sem_r, device_id=(d, g), device_id_type=MESH,
            ).start()
            return 0

        lax.fori_loop(0, NR - 1, go, 0)

    def z_wait(src, dst, sem_r, sem_s):
        n = (NR - 1) * BPS
        c = pltpu.make_async_remote_copy(
            src_ref=src.at[pl.ds(0, n)], dst_ref=dst.at[pl.ds(0, n)],
            send_sem=sem_s, recv_sem=sem_r, device_id=(z_peer(1), g), device_id_type=MESH,
        )
        return c

    def c_send(src, dst, sem_r, sem_s, base=0):
        def go(k, _):
            m = c_peer(k)
            pltpu.make_async_remote_copy(
                src_ref=src.at[m], dst_ref=dst.at[base + me],
                send_sem=sem_s, recv_sem=sem_r, device_id=(r, m * 4 + h), device_id_type=MESH,
            ).start()
            return 0

        lax.fori_loop(1, NQ, go, 0)

    def c_wait(src, dst, sem_r, sem_s):
        return pltpu.make_async_remote_copy(
            src_ref=src.at[pl.ds(0, NQ - 1)], dst_ref=dst.at[pl.ds(0, NQ - 1)],
            send_sem=sem_s, recv_sem=sem_r, device_id=(r, c_peer(1) * 4 + h), device_id_type=MESH,
        )

    def q_send(buf, sem_r, sem_s):
        def go(k, _):
            o = q_peer(k)
            pltpu.make_async_remote_copy(
                src_ref=buf.at[h], dst_ref=buf.at[h],
                send_sem=sem_s, recv_sem=sem_r, device_id=(r, me * 4 + o), device_id_type=MESH,
            ).start()
            return 0

        lax.fori_loop(1, 4, go, 0)

    def q_wait(buf, sem_r, sem_s):
        return pltpu.make_async_remote_copy(
            src_ref=buf.at[pl.ds(0, 3)], dst_ref=buf.at[pl.ds(0, 3)],
            send_sem=sem_s, recv_sem=sem_r, device_id=(r, me * 4 + q_peer(1)), device_id_type=MESH,
        )

    zero = jnp.zeros((8, FB), jnp.float32)

    target = target_ref[...]
    member = jnp.where(iota((16, FD), 0) == target, 1.0, 0.0)
    parts = [member[:, i * FB : (i + 1) * FB] for i in range(FD // FB)]
    stacked = jnp.concatenate(parts, axis=0).astype(jnp.bfloat16)
    lanes = iota((FB, 2 * FB), 1)
    summing = jnp.where((iota((FB, 2 * FB), 0) < lanes) | (lanes >= FB), 1.0, 0.0).astype(jnp.bfloat16)
    sums = jnp.dot(stacked, summing, preferred_element_type=jnp.float32)
    count = jnp.zeros((16, FB), jnp.float32)
    ranks = []
    for i, part in enumerate(parts):
        prefix = sums[16 * i : 16 * i + 16, :FB] + count
        ranks.append(jnp.sum(part * prefix, axis=0, keepdims=True))
        count = count + sums[16 * i : 16 * i + 16, FB:]
    rank = jnp.concatenate(ranks, axis=1).astype(jnp.int32)
    hi = target * BPS + rank // FB
    oh_lo[...] = jnp.where(iota((FB, FD), 0) == rank % FB, 1.0, 0.0).astype(jnp.bfloat16)

    for c in range(NC):
        x = x_ref[pl.ds(8 * c, 8), :]
        big = x.astype(jnp.bfloat16)
        small = (x - big.astype(jnp.float32)).astype(jnp.bfloat16)
        both = jnp.concatenate([big, small], axis=0)
        for b in range(NBLK):
            keep = jnp.where(hi == b, 1.0, 0.0).astype(jnp.bfloat16)
            masked[pl.ds(16 * b, 16), :] = both * keep
        placed = lax.dot_general(
            masked[...], oh_lo[...], (((1,), (1,)), ((), ())), preferred_element_type=jnp.float32
        ).reshape(NBLK, 16, FB)
        zout[c][pl.ds(0, NBLK)] = placed[:, :8] + placed[:, 8:]
        zout[c][NBLK] = zero
        if c == 0:
            pl.semaphore_wait(barrier, (NR - 1) + (NQ - 1) + 3)
        z_send(zout[c], zin[c], sr_z.at[c], ss.at[12 + c])
        zin[c][pl.ds(r * BPS, BPS)] = zout[c][pl.ds(r * BPS, BPS)]
        if c == 0:
            blocks = (count.astype(jnp.int32) + (FB - 1)) // FB
            below = jnp.where(iota((16, 16), 1) < iota((16, 16), 0), 1.0, 0.0).astype(jnp.bfloat16)
            start = jnp.dot(
                below, blocks.astype(jnp.float32).astype(jnp.bfloat16), preferred_element_type=jnp.float32
            )
            base = [jnp.sum(part * start, axis=0, keepdims=True) for part in parts]
            hip_ref[...] = jnp.concatenate(base, axis=1).astype(jnp.int32) + rank // FB
            rows = pair_rows(pairs_ref[:, 0:1], pairs_ref[:, 1:2], owner_ref[...])
            rows = rows + block_rows(start.astype(jnp.int32), blocks)
            bounds = [NBLK - 1, NT - 1, 1, NT, NG - 1, NBLK, NT - 1]
            rows = [jnp.clip(row, 0, high) for row, high in zip(rows, bounds)]
            tabv[...] = jnp.concatenate(rows + [jnp.zeros((1, FB), jnp.int32)], axis=0)
            tab_copy = pltpu.make_async_copy(tabv, tab, tab_sem)
            tab_copy.start()
    tab_copy.wait()

    for t in range(NT):
        for c in range(NC):
            gdo[t // 2, t % 2, c] = zout[c][tab[T_IDX, t]]
    c_send(gdo, gdi, sr_gd, ss.at[1])
    gdi[me] = gdo[me]

    def block_of(ref, u):
        return ref[:, u].reshape(NQ * NC * 8, FB)

    def gram(a, b):
        return lax.dot_general(a, b, (((0,), (0,)), ((), ())), precision=HIGHEST, preferred_element_type=jnp.float32)

    for c in range(NC):
        if c == NC - 1:
            c_wait(gdo, gdi, sr_gd, ss.at[1]).wait_recv()
            for u in range(2):
                xu = block_of(gdi, u)
                qd[h, u] = gram(xu, xu)
            q_send(qd, sr_qd, ss.at[2])
        z_wait(zout[c], zin[c], sr_z.at[c], ss.at[12 + c]).wait_recv()
        for k in range(NQ):
            for u in range(2):
                goo[c][k, u] = zin[c][tab[T_UNIT, u * NQ + k]]
        c_send(goo[c], goi[c], sr_go.at[c], ss.at[15 + c])
        goi[c][me] = goo[c][me]

    q_wait(qd, sr_qd, ss.at[2]).wait_recv()
    eye = jnp.where(
        lax.broadcasted_iota(jnp.int32, (FB, FB), 0) == lax.broadcasted_iota(jnp.int32, (FB, FB), 1), 1.0, 0.0
    )
    for u in range(2):
        m = (qd[0, u] + qd[1, u] + qd[2, u] + qd[3, u]) * (1.0 / COEFFICIENT_SIZE)
        mdo[:, u] = m.reshape(NQ, 8, FB)
        change = jnp.dot(block_of(gdi, u), m - eye, precision=HIGHEST, preferred_element_type=jnp.float32)
        rdo[:, u] = change.reshape(NQ, NC, 8, FB)
    c_send(mdo, mdi, sr_md, ss.at[4])
    mdi[me] = mdo[me]

    for c in range(NC):
        c_wait(goo[c], goi[c], sr_go.at[c], ss.at[15 + c]).wait_recv()
    left = jnp.concatenate([goi[c][:, 0].reshape(NQ * 8, FB) for c in range(NC)], axis=0)
    right = jnp.concatenate([goi[c][:, 1].reshape(NQ * 8, FB) for c in range(NC)], axis=0)
    qo[h] = gram(left, right)
    q_send(qo, sr_qo, ss.at[5])

    c_wait(mdo, mdi, sr_md, ss.at[4]).wait_recv()
    for b in range(NBLK):
        t = tab[T_INV, b]
        mzo[b] = mdi[lax.div(t, 2), lax.rem(t, 2)]
    z_send(mzo, mall, sr_mz, ss.at[6])
    mall[pl.ds(r * BPS, BPS)] = mzo[pl.ds(r * BPS, BPS)]

    q_wait(qo, sr_qo, ss.at[5]).wait_recv()
    m = (qo[0] + qo[1] + qo[2] + qo[3]) * (1.0 / COEFFICIENT_SIZE)
    mko[...] = m.reshape(NQ, 8, FB)
    to_left = lax.dot_general(
        right, m, (((1,), (1,)), ((), ())), precision=HIGHEST, preferred_element_type=jnp.float32
    ).reshape(NC, NQ, 8, FB)
    to_right = jnp.dot(left, m, precision=HIGHEST, preferred_element_type=jnp.float32).reshape(NC, NQ, 8, FB)
    for c in range(NC):
        roo[c][:, 0] = to_left[c]
        roo[c][:, 1] = to_right[c]
        c_send(roo[c], roi[c], sr_ro.at[c], ss.at[18 + c])
        roi[c][me] = roo[c][me]

    c_send(mko, mall, sr_mo, ss.at[8], base=NBLK)
    mall[NBLK + me] = mko[me]
    c_send(rdo, rdi, sr_rd, ss.at[9])
    rdi[me] = rdo[me]

    seg[NT] = zero
    for c in range(NC):
        c_wait(roo[c], roi[c], sr_ro.at[c], ss.at[18 + c]).wait_recv()
        total = zero
        for i in range(NT):
            p = tab[T_PERM, i]
            total = roi[c][lax.rem(p, NQ), lax.div(p, NQ)] + total * tab[T_SAME, i].astype(jnp.float32)
            seg[i] = total
        for b in range(NBLK):
            zro[c][b] = seg[tab[T_LAST, b]]
        z_send(zro[c], zri[c], sr_zr.at[c], ss.at[21 + c])
        zri[c][pl.ds(r * BPS, BPS)] = zro[c][pl.ds(r * BPS, BPS)]
        zri[c][NBLK] = zero

    z_wait(mzo, mall, sr_mz, ss.at[6]).wait_recv()
    c_wait(mko, mall, sr_mo, ss.at[8]).wait_recv()
    for i in range(NQ):
        mfo[i] = mall[tab[T_POS, 4 * i + h]]
    c_send(mfo, mfi, sr_mf, ss.at[11])
    mfi[me] = mfo[me]

    c_wait(rdo, rdi, sr_rd, ss.at[9]).wait_recv()
    hip = hip_ref[...]
    for c in range(NC):
        z_wait(zro[c], zri[c], sr_zr.at[c], ss.at[21 + c]).wait_recv()
        for t in range(PACKED):
            u = gdo[t // 2, t % 2, c] - 0.5 * (rdi[t // 2, t % 2, c] + zri[c][tab[T_IDX, t]])
            big = u.astype(jnp.bfloat16)
            small = (u - big.astype(jnp.float32)).astype(jnp.bfloat16)
            upd[pl.ds(16 * t, 16), :] = jnp.concatenate([big, small], axis=0)
        picked[...] = jnp.dot(upd[...], oh_lo[...], preferred_element_type=jnp.float32)
        total = jnp.zeros((8, FD), jnp.float32)
        for t in range(PACKED):
            both = picked[pl.ds(16 * t, 8), :] + picked[pl.ds(16 * t + 8, 8), :]
            total = total + jnp.where(hip == t, both, 0.0)
        out_ref[pl.ds(8 * c, 8), :] = total

    c_wait(mfo, mfi, sr_mf, ss.at[11]).wait_recv()
    margin_ref[...] = mfi[...].reshape(FB, FB)

    for c in range(NC):
        z_wait(zout[c], zin[c], sr_z.at[c], ss.at[12 + c]).wait_send()
        c_wait(goo[c], goi[c], sr_go.at[c], ss.at[15 + c]).wait_send()
        c_wait(roo[c], roi[c], sr_ro.at[c], ss.at[18 + c]).wait_send()
        z_wait(zro[c], zri[c], sr_zr.at[c], ss.at[21 + c]).wait_send()
    c_wait(gdo, gdi, sr_gd, ss.at[1]).wait_send()
    q_wait(qd, sr_qd, ss.at[2]).wait_send()
    c_wait(mdo, mdi, sr_md, ss.at[4]).wait_send()
    q_wait(qo, sr_qo, ss.at[5]).wait_send()
    z_wait(mzo, mall, sr_mz, ss.at[6]).wait_send()
    c_wait(mko, mall, sr_mo, ss.at[8]).wait_send()
    c_wait(rdo, rdi, sr_rd, ss.at[9]).wait_send()
    c_wait(mfo, mfi, sr_mf, ss.at[11]).wait_send()


def body(coeffs, region_of, block_pairs, block_owner):
    owners = jnp.pad(block_owner, ((0, 0), (0, FB - NG)))
    f32, bf16 = jnp.float32, jnp.bfloat16
    v = pltpu.VMEM
    tile = (8, FB)
    dma = pltpu.SemaphoreType.DMA
    vm = pl.BlockSpec(memory_space=pltpu.VMEM)
    z = [v((NBLK + 1, *tile), f32) for _ in range(NC)]
    pr = [v((NQ, 2, *tile), f32) for _ in range(NC)]
    un = v((NQ, 2, NC, *tile), f32)
    corrected, margin = pl.pallas_call(
        kernel,
        out_shape=(jax.ShapeDtypeStruct((ROWS, FD), f32), jax.ShapeDtypeStruct((FB, FB), f32)),
        in_specs=[vm, vm, vm, vm],
        out_specs=(vm, vm),
        scratch_shapes=[
            v((8, FB), jnp.int32), pltpu.SMEM((8, FB), jnp.int32), v((1, FD), jnp.int32), dma,
            v((FB, FD), bf16), v((NBLK * 16, FD), bf16), z, z, un, un, pr, pr,
            v((4, 2, FB, FB), f32), v((4, FB, FB), f32), un, un, pr, pr, v((NT + 1, *tile), f32), z, z,
            v((NQ, 2, *tile), f32), v((NQ, 2, *tile), f32), v((NBLK, *tile), f32), v((NQ, *tile), f32),
            v((NG, *tile), f32), v((NQ, *tile), f32), v((NQ, *tile), f32),
            v((PACKED * 16, FB), bf16), v((PACKED * 16, FD), f32),
            dma((24,)), dma((NC,)), dma, dma((NC,)), dma, dma, dma, dma((NC,)), dma((NC,)), dma, dma, dma, dma,
        ],
        compiler_params=pltpu.CompilerParams(collective_id=0, has_side_effects=True, vmem_limit_bytes=56 * 2**20),
    )(coeffs, region_of.reshape(1, FD), block_pairs[0], owners)
    return corrected, margin[None, None]


def solution(mesh):
    placed = (P("group", "region"), P("region", None), P("region", None, None), P("region", None))
    return jax.shard_map(
        body,
        mesh=mesh,
        in_specs=placed,
        out_specs=(P("group", "region"), P("region", "group", None, None)),
        check_vma=False,
    )
```

```python
import functools

import jax
import jax.numpy as jnp
from jax import lax
from jax.experimental import pallas as pl
from jax.experimental.pallas import tpu as pltpu
from jax.sharding import PartitionSpec as P

COEFFICIENT_SIZE = 1536
FB = 128
BPS = 4
FD = 2048
NR = 12
NG = 64
NBLK = NR * BPS
NQ = NG // 4
ROWS = 24
NC = ROWS // 8
NT = 2 * NQ
PACKED = 28
ND = PACKED // 2
MESH = pl.DeviceIdType.MESH
HIGHEST = lax.Precision.HIGHEST

T_UNIT, T_PERM, T_SAME, T_LAST, T_POS, T_IDX, T_INV = range(7)


def iota(shape, axis):
    return lax.broadcasted_iota(jnp.int32, shape, axis)


def column(row, n):
    shape = (n, row.shape[1])
    spread = jnp.where(iota(shape, 0) == iota(shape, 1), row, 0)
    return jnp.sum(spread.astype(jnp.float32), axis=1, keepdims=True).astype(jnp.int32)


def pair_rows(left_row, right_row, owner_row):
    left, right = column(left_row, NG), column(right_row, NG)
    lane = iota((NG, FB), 1)
    off = (left != right).astype(jnp.int32)
    off_row = (left_row != right_row).astype(jnp.int32)
    before = jnp.where(iota((NG, NG), 1) < iota((NG, NG), 0), off_row, 0)
    off_rank = jnp.sum(before.astype(jnp.float32), axis=1, keepdims=True).astype(jnp.int32)
    hit = (lane < NT) & (off == 1) & (off_rank == lane % NQ)
    unit = jnp.sum(jnp.where(hit, jnp.where(lane < NQ, left, right), 0), axis=0, keepdims=True)
    u, r = iota((NT, FB), 0), iota((NT, FB), 1)
    dest = column(unit, NT)
    key_row = unit * NT + iota((1, FB), 1)
    key = dest * NT + iota((NT, 1), 0)
    smaller = jnp.where((r < NT) & (key_row < key), 1.0, 0.0)
    rank = jnp.sum(smaller, axis=1, keepdims=True).astype(jnp.int32)
    perm = jnp.sum(jnp.where(rank == r, u, 0), axis=0, keepdims=True)
    here = jnp.sum(jnp.where(rank == r, dest, 0), axis=0, keepdims=True)
    previous = jnp.sum(jnp.where(rank == r - 1, dest, 0), axis=0, keepdims=True)
    same = jnp.where((here == previous) & (iota((1, FB), 1) > 0), 1, 0)
    last = jnp.max(jnp.where(dest == r, rank, -1), axis=0, keepdims=True)
    last = jnp.where(last < 0, NT, last)
    piece = jnp.where(off == 1, NBLK + off_rank, left)
    pos = jnp.sum(jnp.where(column(owner_row, NG) == lane, piece, 0), axis=0, keepdims=True)
    return [unit, perm, same, last, pos]


def block_rows(start, blocks):
    d, t = iota((16, FB), 0), iota((16, FB), 1)
    inside = (t >= start) & (t < start + blocks)
    idx = jnp.sum(jnp.where(inside, d * BPS + t - start + 1, 0), axis=0, keepdims=True) - 1
    idx = jnp.where(idx < 0, NBLK, idx)
    mine = (t // BPS == d) & (t % BPS < blocks)
    inv = jnp.sum(jnp.where(mine, start + t % BPS + 1, 0), axis=0, keepdims=True) - 1
    inv = jnp.where(inv < 0, NT - 1, inv)
    return [idx, inv]


def kernel(
    x_ref, target_ref, pairs_ref, owner_ref, out_ref, margin_ref,
    tabv, tab, hip_ref, tab_sem, oh_lo, masked, zout, zin, gdo, gdi, goo, goi, qd, qo, rdo, rdi, roo, roi, seg, zro, zri,
    mdo, mdi, mzo, mq, mko, moi, mall, mfo, mfi, upd, picked,
    ss, sr_z, sr_gd, sr_go, sr_qd, sr_qo, sr_rd, sr_ro, sr_zr, sr_md, sr_mz, sr_mq, sr_mo, sr_mf,
):
    r = lax.axis_index("region")
    g = lax.axis_index("group")
    me = lax.div(g, 4)
    h = lax.rem(g, 4)

    def z_peer(k):
        return lax.rem(r + k, NR)

    def c_peer(k):
        return lax.rem(me + k, NQ)

    def q_peer(k):
        return lax.rem(h + k, 4)

    barrier = pltpu.get_barrier_semaphore()

    def greet_z(k, _):
        pl.semaphore_signal(barrier, inc=1, device_id=(z_peer(k), g), device_id_type=MESH)
        return 0

    def greet_c(k, _):
        pl.semaphore_signal(barrier, inc=1, device_id=(r, c_peer(k) * 4 + h), device_id_type=MESH)
        return 0

    def greet_q(k, _):
        pl.semaphore_signal(barrier, inc=1, device_id=(r, me * 4 + q_peer(k)), device_id_type=MESH)
        return 0

    lax.fori_loop(1, NR, greet_z, 0)
    lax.fori_loop(1, NQ, greet_c, 0)
    lax.fori_loop(1, 4, greet_q, 0)

    def z_send(src, dst, sem_r, sem_s, n=BPS):
        def go(i, _):
            k = NR // 2 + lax.div(i + 1, 2) * (1 - 2 * lax.rem(i, 2))
            d = z_peer(k)
            pltpu.make_async_remote_copy(
                src_ref=src.at[pl.ds(d * n, n)], dst_ref=dst.at[pl.ds(r * n, n)],
                send_sem=sem_s, recv_sem=sem_r, device_id=(d, g), device_id_type=MESH,
            ).start()
            return 0

        lax.fori_loop(0, NR - 1, go, 0)

    def z_wait(src, dst, sem_r, sem_s, n=BPS):
        n = (NR - 1) * n
        c = pltpu.make_async_remote_copy(
            src_ref=src.at[pl.ds(0, n)], dst_ref=dst.at[pl.ds(0, n)],
            send_sem=sem_s, recv_sem=sem_r, device_id=(z_peer(1), g), device_id_type=MESH,
        )
        return c

    handler = me < ND

    def other_handlers(act):
        @pl.when(handler)
        def _():
            act(ND - 1)

        @pl.when(jnp.logical_not(handler))
        def _():
            act(ND)

    def c_send(src, dst, sem_r, sem_s, only=NQ):
        def go(k, _):
            m = c_peer(k)

            def start():
                pltpu.make_async_remote_copy(
                    src_ref=src.at[m], dst_ref=dst.at[me],
                    send_sem=sem_s, recv_sem=sem_r, device_id=(r, m * 4 + h), device_id_type=MESH,
                ).start()

            if only < NQ:
                pl.when(m < only)(start)
            else:
                start()
            return 0

        lax.fori_loop(1, NQ, go, 0)

    def c_wait(src, dst, sem_r, sem_s, n=NQ - 1):
        return pltpu.make_async_remote_copy(
            src_ref=src.at[pl.ds(0, n)], dst_ref=dst.at[pl.ds(0, n)],
            send_sem=sem_s, recv_sem=sem_r, device_id=(r, c_peer(1) * 4 + h), device_id_type=MESH,
        )

    def q_send(buf, sem_r, sem_s):
        def go(k, _):
            o = q_peer(k)
            pltpu.make_async_remote_copy(
                src_ref=buf.at[h], dst_ref=buf.at[h],
                send_sem=sem_s, recv_sem=sem_r, device_id=(r, me * 4 + o), device_id_type=MESH,
            ).start()
            return 0

        lax.fori_loop(1, 4, go, 0)

    def q_wait(buf, sem_r, sem_s):
        return pltpu.make_async_remote_copy(
            src_ref=buf.at[pl.ds(0, 3)], dst_ref=buf.at[pl.ds(0, 3)],
            send_sem=sem_s, recv_sem=sem_r, device_id=(r, me * 4 + q_peer(1)), device_id_type=MESH,
        )

    zero = jnp.zeros((8, FB), jnp.float32)

    target = target_ref[...]
    member = jnp.where(iota((16, FD), 0) == target, 1.0, 0.0)
    parts = [member[:, i * FB : (i + 1) * FB] for i in range(FD // FB)]
    stacked = jnp.concatenate(parts, axis=0).astype(jnp.bfloat16)
    lanes = iota((FB, 2 * FB), 1)
    summing = jnp.where((iota((FB, 2 * FB), 0) < lanes) | (lanes >= FB), 1.0, 0.0).astype(jnp.bfloat16)
    sums = jnp.dot(stacked, summing, preferred_element_type=jnp.float32)
    count = jnp.zeros((16, FB), jnp.float32)
    ranks = []
    for i, part in enumerate(parts):
        prefix = sums[16 * i : 16 * i + 16, :FB] + count
        ranks.append(jnp.sum(part * prefix, axis=0, keepdims=True))
        count = count + sums[16 * i : 16 * i + 16, FB:]
    rank = jnp.concatenate(ranks, axis=1).astype(jnp.int32)
    hi = target * BPS + rank // FB
    oh_lo[...] = jnp.where(iota((FB, FD), 0) == rank % FB, 1.0, 0.0).astype(jnp.bfloat16)

    for c in range(NC):
        x = x_ref[pl.ds(8 * c, 8), :]
        big = x.astype(jnp.bfloat16)
        small = (x - big.astype(jnp.float32)).astype(jnp.bfloat16)
        both = jnp.concatenate([big, small], axis=0)
        for b in range(NBLK):
            keep = jnp.where(hi == b, 1.0, 0.0).astype(jnp.bfloat16)
            masked[pl.ds(16 * b, 16), :] = both * keep
        placed = lax.dot_general(
            masked[...], oh_lo[...], (((1,), (1,)), ((), ())), preferred_element_type=jnp.float32
        ).reshape(NBLK, 16, FB)
        zout[c][pl.ds(0, NBLK)] = placed[:, :8] + placed[:, 8:]
        zout[c][NBLK] = zero
        if c == 0:
            pl.semaphore_wait(barrier, (NR - 1) + (NQ - 1) + 3)
        z_send(zout[c], zin[c], sr_z.at[c], ss.at[12 + c])
        zin[c][pl.ds(r * BPS, BPS)] = zout[c][pl.ds(r * BPS, BPS)]
        if c == 0:
            blocks = (count.astype(jnp.int32) + (FB - 1)) // FB
            below = jnp.where(iota((16, 16), 1) < iota((16, 16), 0), 1.0, 0.0).astype(jnp.bfloat16)
            start = jnp.dot(
                below, blocks.astype(jnp.float32).astype(jnp.bfloat16), preferred_element_type=jnp.float32
            )
            base = [jnp.sum(part * start, axis=0, keepdims=True) for part in parts]
            hip_ref[...] = jnp.concatenate(base, axis=1).astype(jnp.int32) + rank // FB
            rows = pair_rows(pairs_ref[0:1, :], pairs_ref[1:2, :], owner_ref[...])
            rows = rows + block_rows(start.astype(jnp.int32), blocks)
            bounds = [NBLK - 1, NT - 1, 1, NT, NG - 1, NBLK, NT - 1]
            rows = [jnp.clip(row, 0, high) for row, high in zip(rows, bounds)]
            tabv[...] = jnp.concatenate(rows + [jnp.zeros((1, FB), jnp.int32)], axis=0)
            tab_copy = pltpu.make_async_copy(tabv, tab, tab_sem)
            tab_copy.start()
    tab_copy.wait()

    for t in range(PACKED):
        for c in range(NC):
            gdo[t // 2, t % 2, c] = zout[c][tab[T_IDX, t]]
    c_send(gdo, gdi, sr_gd, ss.at[1], only=ND)
    mdi[NQ - 1, 1] = zero

    def block_of(ref, u):
        return ref[:, u].reshape(NQ * NC * 8, FB)

    def gram(a, b):
        return lax.dot_general(a, b, (((0,), (0,)), ((), ())), precision=HIGHEST, preferred_element_type=jnp.float32)

    for c in range(NC):
        if c == NC - 1:


            @pl.when(handler)
            def _():
                gdi[me] = gdo[me]
                c_wait(gdo, gdi, sr_gd, ss.at[1]).wait_recv()
                for u in range(2):
                    xu = block_of(gdi, u)
                    qd[h, u] = gram(xu, xu)
                q_send(qd, sr_qd, ss.at[2])

        z_wait(zout[c], zin[c], sr_z.at[c], ss.at[12 + c]).wait_recv()
        for k in range(NQ):
            for u in range(2):
                goo[c][k, u] = zin[c][tab[T_UNIT, u * NQ + k]]
        c_send(goo[c], goi[c], sr_go.at[c], ss.at[15 + c])
        goi[c][me] = goo[c][me]

    @pl.when(handler)
    def _():
        q_wait(qd, sr_qd, ss.at[2]).wait_recv()
        eye = jnp.where(iota((FB, FB), 0) == iota((FB, FB), 1), 1.0, 0.0)
        for u in range(2):
            m = (qd[0, u] + qd[1, u] + qd[2, u] + qd[3, u]) * (1.0 / COEFFICIENT_SIZE)
            mdo[:, u] = m.reshape(NQ, 8, FB)
            change = jnp.dot(block_of(gdi, u), m - eye, precision=HIGHEST, preferred_element_type=jnp.float32)
            rdo[:, u] = change.reshape(NQ, NC, 8, FB)
        c_send(mdo, mdi, sr_md, ss.at[4])
        mdi[me] = mdo[me]

    for c in range(NC):
        c_wait(goo[c], goi[c], sr_go.at[c], ss.at[15 + c]).wait_recv()
    left = jnp.concatenate([goi[c][:, 0].reshape(NQ * 8, FB) for c in range(NC)], axis=0)
    right = jnp.concatenate([goi[c][:, 1].reshape(NQ * 8, FB) for c in range(NC)], axis=0)
    qo[h] = gram(left, right)
    q_send(qo, sr_qo, ss.at[5])

    other_handlers(lambda n: c_wait(mdo, mdi, sr_md, ss.at[4], n).wait_recv())
    for d in range(NR):
        t = tab[T_INV, d * BPS + h]
        mzo[d] = mdi[lax.div(t, 2), lax.rem(t, 2)]
    z_send(mzo, mq.at[h], sr_mz, ss.at[6], 1)
    mq[h, r] = mzo[r]

    q_wait(qo, sr_qo, ss.at[5]).wait_recv()
    m = (qo[0] + qo[1] + qo[2] + qo[3]) * (1.0 / COEFFICIENT_SIZE)
    mko[...] = m.reshape(NQ, 8, FB)
    to_left = lax.dot_general(
        right, m, (((1,), (1,)), ((), ())), precision=HIGHEST, preferred_element_type=jnp.float32
    ).reshape(NC, NQ, 8, FB)
    to_right = jnp.dot(left, m, precision=HIGHEST, preferred_element_type=jnp.float32).reshape(NC, NQ, 8, FB)
    for c in range(NC):
        roo[c][:, 0] = to_left[c]
        roo[c][:, 1] = to_right[c]
        c_send(roo[c], roi[c], sr_ro.at[c], ss.at[18 + c])
        roi[c][me] = roo[c][me]

    c_send(mko, moi, sr_mo, ss.at[8])
    moi[me] = mko[me]

    @pl.when(handler)
    def _():
        c_send(rdo, rdi, sr_rd, ss.at[9])
        rdi[me] = rdo[me]

    seg[NT] = zero
    for c in range(NC):
        c_wait(roo[c], roi[c], sr_ro.at[c], ss.at[18 + c]).wait_recv()
        total = zero
        for i in range(NT):
            p = tab[T_PERM, i]
            total = roi[c][lax.rem(p, NQ), lax.div(p, NQ)] + total * tab[T_SAME, i].astype(jnp.float32)
            seg[i] = total
        for b in range(NBLK):
            zro[c][b] = seg[tab[T_LAST, b]]
        z_send(zro[c], zri[c], sr_zr.at[c], ss.at[21 + c])
        zri[c][pl.ds(r * BPS, BPS)] = zro[c][pl.ds(r * BPS, BPS)]
        zri[c][NBLK] = zero

    z_wait(mzo, mq.at[h], sr_mz, ss.at[6], 1).wait_recv()
    q_send(mq, sr_mq, ss.at[0])
    c_wait(mko, moi, sr_mo, ss.at[8]).wait_recv()
    q_wait(mq, sr_mq, ss.at[0]).wait_recv()
    for b in range(NBLK):
        mall[b] = mq[b % BPS, b // BPS]
    mall[pl.ds(NBLK, NQ)] = moi[...]
    for i in range(NQ):
        mfo[i] = mall[tab[T_POS, 4 * i + h]]
    c_send(mfo, mfi, sr_mf, ss.at[11])
    mfi[me] = mfo[me]

    other_handlers(lambda n: c_wait(rdo, rdi, sr_rd, ss.at[9], n).wait_recv())
    hip = hip_ref[...]
    for c in range(NC):
        z_wait(zro[c], zri[c], sr_zr.at[c], ss.at[21 + c]).wait_recv()
        for t in range(PACKED):
            u = gdo[t // 2, t % 2, c] - 0.5 * (rdi[t // 2, t % 2, c] + zri[c][tab[T_IDX, t]])
            big = u.astype(jnp.bfloat16)
            small = (u - big.astype(jnp.float32)).astype(jnp.bfloat16)
            upd[pl.ds(16 * t, 16), :] = jnp.concatenate([big, small], axis=0)
        picked[...] = jnp.dot(upd[...], oh_lo[...], preferred_element_type=jnp.float32)
        total = jnp.zeros((8, FD), jnp.float32)
        for t in range(PACKED):
            both = picked[pl.ds(16 * t, 8), :] + picked[pl.ds(16 * t + 8, 8), :]
            total = total + jnp.where(hip == t, both, 0.0)
        out_ref[pl.ds(8 * c, 8), :] = total

    c_wait(mfo, mfi, sr_mf, ss.at[11]).wait_recv()
    margin_ref[...] = mfi[...].reshape(FB, FB)

    for c in range(NC):
        z_wait(zout[c], zin[c], sr_z.at[c], ss.at[12 + c]).wait_send()
        c_wait(goo[c], goi[c], sr_go.at[c], ss.at[15 + c]).wait_send()
        c_wait(roo[c], roi[c], sr_ro.at[c], ss.at[18 + c]).wait_send()
        z_wait(zro[c], zri[c], sr_zr.at[c], ss.at[21 + c]).wait_send()
    other_handlers(lambda n: c_wait(gdo, gdi, sr_gd, ss.at[1], n).wait_send())

    @pl.when(handler)
    def _():
        q_wait(qd, sr_qd, ss.at[2]).wait_send()
        c_wait(mdo, mdi, sr_md, ss.at[4]).wait_send()
        c_wait(rdo, rdi, sr_rd, ss.at[9]).wait_send()

    q_wait(qo, sr_qo, ss.at[5]).wait_send()
    z_wait(mzo, mq.at[h], sr_mz, ss.at[6], 1).wait_send()
    c_wait(mko, moi, sr_mo, ss.at[8]).wait_send()
    q_wait(mq, sr_mq, ss.at[0]).wait_send()
    c_wait(mfo, mfi, sr_mf, ss.at[11]).wait_send()


def body(coeffs, region_of, block_pairs, block_owner):
    f32, bf16 = jnp.float32, jnp.bfloat16
    v = pltpu.VMEM
    tile = (8, FB)
    dma = pltpu.SemaphoreType.DMA
    vm = pl.BlockSpec(memory_space=pltpu.VMEM)
    z = [v((NBLK + 1, *tile), f32) for _ in range(NC)]
    pr = [v((NQ, 2, *tile), f32) for _ in range(NC)]
    un = v((NQ, 2, NC, *tile), f32)
    corrected, margin = pl.pallas_call(
        kernel,
        out_shape=(jax.ShapeDtypeStruct((ROWS, FD), f32), jax.ShapeDtypeStruct((FB, FB), f32)),
        in_specs=[vm, vm, vm, vm],
        out_specs=(vm, vm),
        scratch_shapes=[
            v((8, FB), jnp.int32), pltpu.SMEM((8, FB), jnp.int32), v((1, FD), jnp.int32), dma,
            v((FB, FD), bf16), v((NBLK * 16, FD), bf16), z, z, un, un, pr, pr,
            v((4, 2, FB, FB), f32), v((4, FB, FB), f32), un, un, pr, pr, v((NT + 1, *tile), f32), z, z,
            v((NQ, 2, *tile), f32), v((NQ, 2, *tile), f32), v((NR, *tile), f32), v((4, NR, *tile), f32),
            v((NQ, *tile), f32), v((NQ, *tile), f32), v((NG, *tile), f32), v((NQ, *tile), f32), v((NQ, *tile), f32),
            v((PACKED * 16, FB), bf16), v((PACKED * 16, FD), f32),
            dma((24,)), dma((NC,)), dma, dma((NC,)), dma, dma, dma, dma((NC,)), dma((NC,)), dma, dma, dma, dma, dma,
        ],
        compiler_params=pltpu.CompilerParams(collective_id=0, has_side_effects=True, vmem_limit_bytes=56 * 2**20),
    )(coeffs, region_of.reshape(1, FD), block_pairs[0].T, block_owner)
    return corrected, margin[None, None]


def solution(mesh):
    placed = (P("group", "region"), P("region", None), P("region", None, None), P("region", None))
    return jax.shard_map(
        body,
        mesh=mesh,
        in_specs=placed,
        out_specs=(P("group", "region"), P("region", "group", None, None)),
        check_vma=False,
    )
```

```python
import functools

import jax
import jax.numpy as jnp
from jax import lax
from jax.experimental import pallas as pl
from jax.experimental.pallas import tpu as pltpu
from jax.sharding import PartitionSpec as P

COEFFICIENT_SIZE = 1536
FB = 128
BPS = 4
FD = 2048
NR = 12
NG = 64
NBLK = NR * BPS
NQ = NG // 4
ROWS = 24
NC = ROWS // 8
NT = 2 * NQ
PACKED = 28
ND = PACKED // 2
MESH = pl.DeviceIdType.MESH
HIGHEST = lax.Precision.HIGHEST

T_UNIT, T_PERM, T_SAME, T_LAST, T_POS, T_IDX, T_INV = range(7)


def iota(shape, axis):
    return lax.broadcasted_iota(jnp.int32, shape, axis)


def column(row, n):
    shape = (n, row.shape[1])
    spread = jnp.where(iota(shape, 0) == iota(shape, 1), row, 0)
    return jnp.sum(spread.astype(jnp.float32), axis=1, keepdims=True).astype(jnp.int32)


def pair_rows(left_row, right_row, owner_row):
    left, right = column(left_row, NG), column(right_row, NG)
    lane = iota((NG, FB), 1)
    off = (left != right).astype(jnp.int32)
    off_row = (left_row != right_row).astype(jnp.int32)
    before = jnp.where(iota((NG, NG), 1) < iota((NG, NG), 0), off_row, 0)
    off_rank = jnp.sum(before.astype(jnp.float32), axis=1, keepdims=True).astype(jnp.int32)
    hit = (lane < NT) & (off == 1) & (off_rank == lane % NQ)
    unit = jnp.sum(jnp.where(hit, jnp.where(lane < NQ, left, right), 0), axis=0, keepdims=True)
    u, r = iota((NT, FB), 0), iota((NT, FB), 1)
    dest = column(unit, NT)
    key_row = unit * NT + iota((1, FB), 1)
    key = dest * NT + iota((NT, 1), 0)
    smaller = jnp.where((r < NT) & (key_row < key), 1.0, 0.0)
    rank = jnp.sum(smaller, axis=1, keepdims=True).astype(jnp.int32)
    perm = jnp.sum(jnp.where(rank == r, u, 0), axis=0, keepdims=True)
    here = jnp.sum(jnp.where(rank == r, dest, 0), axis=0, keepdims=True)
    previous = jnp.sum(jnp.where(rank == r - 1, dest, 0), axis=0, keepdims=True)
    same = jnp.where((here == previous) & (iota((1, FB), 1) > 0), 1, 0)
    last = jnp.max(jnp.where(dest == r, rank, -1), axis=0, keepdims=True)
    last = jnp.where(last < 0, NT, last)
    piece = jnp.where(off == 1, NBLK + off_rank, left)
    pos = jnp.sum(jnp.where(column(owner_row, NG) == lane, piece, 0), axis=0, keepdims=True)
    return [unit, perm, same, last, pos]


def block_rows(start, blocks):
    d, t = iota((16, FB), 0), iota((16, FB), 1)
    inside = (t >= start) & (t < start + blocks)
    idx = jnp.sum(jnp.where(inside, d * BPS + t - start + 1, 0), axis=0, keepdims=True) - 1
    idx = jnp.where(idx < 0, NBLK, idx)
    mine = (t // BPS == d) & (t % BPS < blocks)
    inv = jnp.sum(jnp.where(mine, start + t % BPS + 1, 0), axis=0, keepdims=True) - 1
    inv = jnp.where(inv < 0, NT - 1, inv)
    return [idx, inv]


def kernel(
    x_ref, target_ref, pairs_ref, owner_ref, big_ref, small_ref, margin_ref,
    tabv, tab, hip_ref, tab_sem, oh_lo, masked, zout, zin, gdo, gdi, goo, goi, qd, qo, rdo, rdi, roo, roi, seg, zro, zri,
    mdo, mdi, mzo, mq, mko, moi, mall, mfo, mfi, upd, picked,
    ss, sr_z, sr_gd, sr_go, sr_qd, sr_qo, sr_rd, sr_ro, sr_zr, sr_md, sr_mz, sr_mq, sr_mo, sr_mf,
):
    r = lax.axis_index("region")
    g = lax.axis_index("group")
    me = lax.div(g, 4)
    h = lax.rem(g, 4)

    def z_peer(k):
        return lax.rem(r + k, NR)

    def c_peer(k):
        return lax.rem(me + k, NQ)

    def q_peer(k):
        return lax.rem(h + k, 4)

    barrier = pltpu.get_barrier_semaphore()

    def greet_z(k, _):
        pl.semaphore_signal(barrier, inc=1, device_id=(z_peer(k), g), device_id_type=MESH)
        return 0

    def greet_c(k, _):
        pl.semaphore_signal(barrier, inc=1, device_id=(r, c_peer(k) * 4 + h), device_id_type=MESH)
        return 0

    def greet_q(k, _):
        pl.semaphore_signal(barrier, inc=1, device_id=(r, me * 4 + q_peer(k)), device_id_type=MESH)
        return 0

    lax.fori_loop(1, NR, greet_z, 0)
    lax.fori_loop(1, NQ, greet_c, 0)
    lax.fori_loop(1, 4, greet_q, 0)

    def z_send(src, dst, sem_r, sem_s, n=BPS):
        def go(i, _):
            k = NR // 2 + lax.div(i + 1, 2) * (1 - 2 * lax.rem(i, 2))
            d = z_peer(k)
            pltpu.make_async_remote_copy(
                src_ref=src.at[pl.ds(d * n, n)], dst_ref=dst.at[pl.ds(r * n, n)],
                send_sem=sem_s, recv_sem=sem_r, device_id=(d, g), device_id_type=MESH,
            ).start()
            return 0

        lax.fori_loop(0, NR - 1, go, 0)

    def z_wait(src, dst, sem_r, sem_s, n=BPS):
        n = (NR - 1) * n
        c = pltpu.make_async_remote_copy(
            src_ref=src.at[pl.ds(0, n)], dst_ref=dst.at[pl.ds(0, n)],
            send_sem=sem_s, recv_sem=sem_r, device_id=(z_peer(1), g), device_id_type=MESH,
        )
        return c

    handler = me < ND

    def other_handlers(act):
        @pl.when(handler)
        def _():
            act(ND - 1)

        @pl.when(jnp.logical_not(handler))
        def _():
            act(ND)

    def c_send(src, dst, sem_r, sem_s, only=NQ):
        def go(k, _):
            m = c_peer(k)

            def start():
                pltpu.make_async_remote_copy(
                    src_ref=src.at[m], dst_ref=dst.at[me],
                    send_sem=sem_s, recv_sem=sem_r, device_id=(r, m * 4 + h), device_id_type=MESH,
                ).start()

            if only < NQ:
                pl.when(m < only)(start)
            else:
                start()
            return 0

        lax.fori_loop(1, NQ, go, 0)

    def c_wait(src, dst, sem_r, sem_s, n=NQ - 1):
        return pltpu.make_async_remote_copy(
            src_ref=src.at[pl.ds(0, n)], dst_ref=dst.at[pl.ds(0, n)],
            send_sem=sem_s, recv_sem=sem_r, device_id=(r, c_peer(1) * 4 + h), device_id_type=MESH,
        )

    def q_send(buf, sem_r, sem_s):
        def go(k, _):
            o = q_peer(k)
            pltpu.make_async_remote_copy(
                src_ref=buf.at[h], dst_ref=buf.at[h],
                send_sem=sem_s, recv_sem=sem_r, device_id=(r, me * 4 + o), device_id_type=MESH,
            ).start()
            return 0

        lax.fori_loop(1, 4, go, 0)

    def q_wait(buf, sem_r, sem_s):
        return pltpu.make_async_remote_copy(
            src_ref=buf.at[pl.ds(0, 3)], dst_ref=buf.at[pl.ds(0, 3)],
            send_sem=sem_s, recv_sem=sem_r, device_id=(r, me * 4 + q_peer(1)), device_id_type=MESH,
        )

    zero = jnp.zeros((8, FB), jnp.float32)

    target = target_ref[...]
    member = jnp.where(iota((16, FD), 0) == target, 1.0, 0.0)
    parts = [member[:, i * FB : (i + 1) * FB] for i in range(FD // FB)]
    stacked = jnp.concatenate(parts, axis=0).astype(jnp.bfloat16)
    lanes = iota((FB, 2 * FB), 1)
    summing = jnp.where((iota((FB, 2 * FB), 0) < lanes) | (lanes >= FB), 1.0, 0.0).astype(jnp.bfloat16)
    sums = jnp.dot(stacked, summing, preferred_element_type=jnp.float32)
    count = jnp.zeros((16, FB), jnp.float32)
    ranks = []
    for i, part in enumerate(parts):
        prefix = sums[16 * i : 16 * i + 16, :FB] + count
        ranks.append(jnp.sum(part * prefix, axis=0, keepdims=True))
        count = count + sums[16 * i : 16 * i + 16, FB:]
    rank = jnp.concatenate(ranks, axis=1).astype(jnp.int32)
    hi = target * BPS + rank // FB
    oh_lo[...] = jnp.where(iota((FB, FD), 0) == rank % FB, 1.0, 0.0).astype(jnp.bfloat16)

    for c in range(NC):
        x = x_ref[pl.ds(8 * c, 8), :]
        big = x.astype(jnp.bfloat16)
        small = (x - big.astype(jnp.float32)).astype(jnp.bfloat16)
        both = jnp.concatenate([big, small], axis=0)
        for b in range(NBLK):
            keep = jnp.where(hi == b, 1.0, 0.0).astype(jnp.bfloat16)
            masked[pl.ds(16 * b, 16), :] = both * keep
        placed = lax.dot_general(
            masked[...], oh_lo[...], (((1,), (1,)), ((), ())), preferred_element_type=jnp.float32
        ).reshape(NBLK, 16, FB)
        zout[c][pl.ds(0, NBLK)] = placed[:, :8] + placed[:, 8:]
        zout[c][NBLK] = zero
        if c == 0:
            pl.semaphore_wait(barrier, (NR - 1) + (NQ - 1) + 3)
        z_send(zout[c], zin[c], sr_z.at[c], ss.at[12 + c])
        zin[c][pl.ds(r * BPS, BPS)] = zout[c][pl.ds(r * BPS, BPS)]
        if c == 0:
            blocks = (count.astype(jnp.int32) + (FB - 1)) // FB
            below = jnp.where(iota((16, 16), 1) < iota((16, 16), 0), 1.0, 0.0).astype(jnp.bfloat16)
            start = jnp.dot(
                below, blocks.astype(jnp.float32).astype(jnp.bfloat16), preferred_element_type=jnp.float32
            )
            base = [jnp.sum(part * start, axis=0, keepdims=True) for part in parts]
            hip_ref[...] = jnp.concatenate(base, axis=1).astype(jnp.int32) + rank // FB
            rows = pair_rows(pairs_ref[0:1, :], pairs_ref[1:2, :], owner_ref[...])
            rows = rows + block_rows(start.astype(jnp.int32), blocks)
            bounds = [NBLK - 1, NT - 1, 1, NT, NG - 1, NBLK, NT - 1]
            rows = [jnp.clip(row, 0, high) for row, high in zip(rows, bounds)]
            tabv[...] = jnp.concatenate(rows + [jnp.zeros((1, FB), jnp.int32)], axis=0)
            tab_copy = pltpu.make_async_copy(tabv, tab, tab_sem)
            tab_copy.start()
    tab_copy.wait()

    for t in range(PACKED):
        for c in range(NC):
            gdo[t // 2, t % 2, c] = zout[c][tab[T_IDX, t]]
    c_send(gdo, gdi, sr_gd, ss.at[1], only=ND)
    mdi[NQ - 1, 1] = zero

    def block_of(ref, u):
        return ref[:, u].reshape(NQ * NC * 8, FB)

    def gram(a, b):
        return lax.dot_general(a, b, (((0,), (0,)), ((), ())), precision=HIGHEST, preferred_element_type=jnp.float32)

    for c in range(NC):
        if c == NC - 1:


            @pl.when(handler)
            def _():
                gdi[me] = gdo[me]
                c_wait(gdo, gdi, sr_gd, ss.at[1]).wait_recv()
                for u in range(2):
                    xu = block_of(gdi, u)
                    qd[h, u] = gram(xu, xu)
                q_send(qd, sr_qd, ss.at[2])

        z_wait(zout[c], zin[c], sr_z.at[c], ss.at[12 + c]).wait_recv()
        for k in range(NQ):
            for u in range(2):
                goo[c][k, u] = zin[c][tab[T_UNIT, u * NQ + k]]
        c_send(goo[c], goi[c], sr_go.at[c], ss.at[15 + c])
        goi[c][me] = goo[c][me]

    @pl.when(handler)
    def _():
        q_wait(qd, sr_qd, ss.at[2]).wait_recv()
        eye = jnp.where(iota((FB, FB), 0) == iota((FB, FB), 1), 1.0, 0.0)
        for u in range(2):
            m = qd[0, u] + qd[1, u] + qd[2, u] + qd[3, u]
            mdo[:, u] = m.reshape(NQ, 8, FB)
            shift = m * (1.0 / COEFFICIENT_SIZE) - eye
            change = jnp.dot(block_of(gdi, u), shift, precision=HIGHEST, preferred_element_type=jnp.float32)
            rdo[:, u] = change.reshape(NQ, NC, 8, FB)
        c_send(mdo, mdi, sr_md, ss.at[4])
        mdi[me] = mdo[me]

    total = None
    for c in range(NC):
        c_wait(goo[c], goi[c], sr_go.at[c], ss.at[15 + c]).wait_recv()
        part = gram(goi[c][:, 0].reshape(NQ * 8, FB), goi[c][:, 1].reshape(NQ * 8, FB))
        total = part if total is None else total + part
    qo[h] = total
    q_send(qo, sr_qo, ss.at[5])

    other_handlers(lambda n: c_wait(mdo, mdi, sr_md, ss.at[4], n).wait_recv())
    for d in range(NR):
        t = tab[T_INV, d * BPS + h]
        mzo[d] = mdi[lax.div(t, 2), lax.rem(t, 2)]
    z_send(mzo, mq.at[h], sr_mz, ss.at[6], 1)
    mq[h, r] = mzo[r]

    q_wait(qo, sr_qo, ss.at[5]).wait_recv()
    m = qo[0] + qo[1] + qo[2] + qo[3]
    mko[...] = m.reshape(NQ, 8, FB)
    m = m * (1.0 / COEFFICIENT_SIZE)
    for c in range(NC):
        lc, rc = goi[c][:, 0].reshape(NQ * 8, FB), goi[c][:, 1].reshape(NQ * 8, FB)
        to_left = lax.dot_general(
            rc, m, (((1,), (1,)), ((), ())), precision=HIGHEST, preferred_element_type=jnp.float32
        )
        roo[c][:, 0] = to_left.reshape(NQ, 8, FB)
        roo[c][:, 1] = jnp.dot(lc, m, precision=HIGHEST, preferred_element_type=jnp.float32).reshape(NQ, 8, FB)
        c_send(roo[c], roi[c], sr_ro.at[c], ss.at[18 + c])
        roi[c][me] = roo[c][me]

    c_send(mko, moi, sr_mo, ss.at[8])
    moi[me] = mko[me]

    @pl.when(handler)
    def _():
        c_send(rdo, rdi, sr_rd, ss.at[9])
        rdi[me] = rdo[me]

    seg[NT] = zero
    for c in range(NC):
        c_wait(roo[c], roi[c], sr_ro.at[c], ss.at[18 + c]).wait_recv()
        total = zero
        for i in range(NT):
            p = tab[T_PERM, i]
            total = roi[c][lax.rem(p, NQ), lax.div(p, NQ)] + total * tab[T_SAME, i].astype(jnp.float32)
            seg[i] = total
        for b in range(NBLK):
            zro[c][b] = seg[tab[T_LAST, b]]
        z_send(zro[c], zri[c], sr_zr.at[c], ss.at[21 + c])
        zri[c][pl.ds(r * BPS, BPS)] = zro[c][pl.ds(r * BPS, BPS)]
        zri[c][NBLK] = zero

    z_wait(mzo, mq.at[h], sr_mz, ss.at[6], 1).wait_recv()
    q_send(mq, sr_mq, ss.at[0])
    c_wait(mko, moi, sr_mo, ss.at[8]).wait_recv()
    q_wait(mq, sr_mq, ss.at[0]).wait_recv()
    for b in range(NBLK):
        mall[b] = mq[b % BPS, b // BPS]
    mall[pl.ds(NBLK, NQ)] = moi[...]
    for i in range(NQ):
        mfo[i] = mall[tab[T_POS, 4 * i + h]]
    c_send(mfo, mfi, sr_mf, ss.at[11])
    mfi[me] = mfo[me]

    other_handlers(lambda n: c_wait(rdo, rdi, sr_rd, ss.at[9], n).wait_recv())
    hip = hip_ref[...]
    for c in range(NC):
        z_wait(zro[c], zri[c], sr_zr.at[c], ss.at[21 + c]).wait_recv()
        for t in range(PACKED):
            u = gdo[t // 2, t % 2, c] - 0.5 * (rdi[t // 2, t % 2, c] + zri[c][tab[T_IDX, t]])
            big = u.astype(jnp.bfloat16)
            small = (u - big.astype(jnp.float32)).astype(jnp.bfloat16)
            upd[pl.ds(16 * t, 16), :] = jnp.concatenate([big, small], axis=0)
        picked[...] = jnp.dot(upd[...], oh_lo[...], preferred_element_type=jnp.float32)
        for part, ref in enumerate((big_ref, small_ref)):
            total = jnp.zeros((8, FD), jnp.float32)
            for t in range(PACKED):
                total = total + jnp.where(hip == t, picked[pl.ds(16 * t + 8 * part, 8), :], 0.0)
            ref[pl.ds(8 * c, 8), :] = total

    c_wait(mfo, mfi, sr_mf, ss.at[11]).wait_recv()
    margin_ref[...] = mfi[...].reshape(FB, FB)

    for c in range(NC):
        z_wait(zout[c], zin[c], sr_z.at[c], ss.at[12 + c]).wait_send()
        c_wait(goo[c], goi[c], sr_go.at[c], ss.at[15 + c]).wait_send()
        c_wait(roo[c], roi[c], sr_ro.at[c], ss.at[18 + c]).wait_send()
        z_wait(zro[c], zri[c], sr_zr.at[c], ss.at[21 + c]).wait_send()
    other_handlers(lambda n: c_wait(gdo, gdi, sr_gd, ss.at[1], n).wait_send())

    @pl.when(handler)
    def _():
        q_wait(qd, sr_qd, ss.at[2]).wait_send()
        c_wait(mdo, mdi, sr_md, ss.at[4]).wait_send()
        c_wait(rdo, rdi, sr_rd, ss.at[9]).wait_send()

    q_wait(qo, sr_qo, ss.at[5]).wait_send()
    z_wait(mzo, mq.at[h], sr_mz, ss.at[6], 1).wait_send()
    c_wait(mko, moi, sr_mo, ss.at[8]).wait_send()
    q_wait(mq, sr_mq, ss.at[0]).wait_send()
    c_wait(mfo, mfi, sr_mf, ss.at[11]).wait_send()


def body(coeffs, region_of, block_pairs, block_owner):
    f32, bf16 = jnp.float32, jnp.bfloat16
    v = pltpu.VMEM
    tile = (8, FB)
    dma = pltpu.SemaphoreType.DMA
    vm = pl.BlockSpec(memory_space=pltpu.VMEM)
    z = [v((NBLK + 1, *tile), f32) for _ in range(NC)]
    pr = [v((NQ, 2, *tile), f32) for _ in range(NC)]
    un = v((NQ, 2, NC, *tile), f32)
    big, small, margin = pl.pallas_call(
        kernel,
        out_shape=(
            jax.ShapeDtypeStruct((ROWS, FD), f32),
            jax.ShapeDtypeStruct((ROWS, FD), f32),
            jax.ShapeDtypeStruct((FB, FB), f32),
        ),
        in_specs=[vm, vm, vm, vm],
        out_specs=(vm, vm, vm),
        scratch_shapes=[
            v((8, FB), jnp.int32), pltpu.SMEM((8, FB), jnp.int32), v((1, FD), jnp.int32), dma,
            v((FB, FD), bf16), v((NBLK * 16, FD), bf16), z, z, un, un, pr, pr,
            v((4, 2, FB, FB), f32), v((4, FB, FB), f32), un, un, pr, pr, v((NT + 1, *tile), f32), z, z,
            v((NQ, 2, *tile), f32), v((NQ, 2, *tile), f32), v((NR, *tile), f32), v((4, NR, *tile), f32),
            v((NQ, *tile), f32), v((NQ, *tile), f32), v((NG, *tile), f32), v((NQ, *tile), f32), v((NQ, *tile), f32),
            v((PACKED * 16, FB), bf16), v((PACKED * 16, FD), f32),
            dma((24,)), dma((NC,)), dma, dma((NC,)), dma, dma, dma, dma((NC,)), dma((NC,)), dma, dma, dma, dma, dma,
        ],
        compiler_params=pltpu.CompilerParams(collective_id=0, has_side_effects=True, vmem_limit_bytes=56 * 2**20),
    )(coeffs, region_of.reshape(1, FD), block_pairs[0].T, block_owner)
    return big + small, (margin * (1.0 / COEFFICIENT_SIZE))[None, None]


def solution(mesh):
    placed = (P("group", "region"), P("region", None), P("region", None, None), P("region", None))
    return jax.shard_map(
        body,
        mesh=mesh,
        in_specs=placed,
        out_specs=(P("group", "region"), P("region", "group", None, None)),
        check_vma=False,
    )
```

```python
import functools

import jax
import jax.numpy as jnp
from jax import lax
from jax.experimental import pallas as pl
from jax.experimental.pallas import tpu as pltpu
from jax.sharding import PartitionSpec as P

COEFFICIENT_SIZE = 1536
FB = 128
BPS = 4
FD = 2048
NR = 12
NG = 64
NBLK = NR * BPS
NQ = NG // 4
ROWS = 24
NC = ROWS // 8
NT = 2 * NQ
PACKED = 28
ND = PACKED // 2
MESH = pl.DeviceIdType.MESH
HIGHEST = lax.Precision.HIGHEST

T_UNIT, T_PERM, T_SAME, T_LAST, T_POS, T_IDX, T_INV = range(7)


def iota(shape, axis):
    return lax.broadcasted_iota(jnp.int32, shape, axis)


def column(row, n):
    shape = (n, row.shape[1])
    spread = jnp.where(iota(shape, 0) == iota(shape, 1), row, 0)
    return jnp.sum(spread.astype(jnp.float32), axis=1, keepdims=True).astype(jnp.int32)


def pair_rows(left_row, right_row, owner_row):
    left, right = column(left_row, NG), column(right_row, NG)
    lane = iota((NG, FB), 1)
    off = (left != right).astype(jnp.int32)
    off_row = (left_row != right_row).astype(jnp.int32)
    before = jnp.where(iota((NG, NG), 1) < iota((NG, NG), 0), off_row, 0)
    off_rank = jnp.sum(before.astype(jnp.float32), axis=1, keepdims=True).astype(jnp.int32)
    hit = (lane < NT) & (off == 1) & (off_rank == lane % NQ)
    unit = jnp.sum(jnp.where(hit, jnp.where(lane < NQ, left, right), 0), axis=0, keepdims=True)
    u, r = iota((NT, FB), 0), iota((NT, FB), 1)
    dest = column(unit, NT)
    key_row = unit * NT + iota((1, FB), 1)
    key = dest * NT + iota((NT, 1), 0)
    smaller = jnp.where((r < NT) & (key_row < key), 1.0, 0.0)
    rank = jnp.sum(smaller, axis=1, keepdims=True).astype(jnp.int32)
    perm = jnp.sum(jnp.where(rank == r, u, 0), axis=0, keepdims=True)
    here = jnp.sum(jnp.where(rank == r, dest, 0), axis=0, keepdims=True)
    previous = jnp.sum(jnp.where(rank == r - 1, dest, 0), axis=0, keepdims=True)
    same = jnp.where((here == previous) & (iota((1, FB), 1) > 0), 1, 0)
    last = jnp.max(jnp.where(dest == r, rank, -1), axis=0, keepdims=True)
    last = jnp.where(last < 0, NT, last)
    piece = jnp.where(off == 1, NBLK + off_rank, left)
    pos = jnp.sum(jnp.where(column(owner_row, NG) == lane, piece, 0), axis=0, keepdims=True)
    return [unit, perm, same, last, pos]


def block_rows(start, blocks):
    d, t = iota((16, FB), 0), iota((16, FB), 1)
    inside = (t >= start) & (t < start + blocks)
    idx = jnp.sum(jnp.where(inside, d * BPS + t - start + 1, 0), axis=0, keepdims=True) - 1
    idx = jnp.where(idx < 0, NBLK, idx)
    mine = (t // BPS == d) & (t % BPS < blocks)
    inv = jnp.sum(jnp.where(mine, start + t % BPS + 1, 0), axis=0, keepdims=True) - 1
    inv = jnp.where(inv < 0, NT - 1, inv)
    return [idx, inv]


def kernel(
    x_ref, target_ref, pairs_ref, owner_ref, big_ref, small_ref, margin_ref,
    tabv, tab, hip_ref, tab_sem, oh_lo, masked, zout, zin, gdo, gdi, goo, goi, qd, qo, rdo, rdi, roo, roi, seg, zro, zri,
    mdo, mdi, mzo, mq, mko, moi, mall, mfo, mfi, upd, picked,
    ss, sr_z, sr_gd, sr_go, sr_qd, sr_qo, sr_rd, sr_ro, sr_zr, sr_md, sr_mz, sr_mq, sr_mo, sr_mf,
):
    r = lax.axis_index("region")
    g = lax.axis_index("group")
    me = lax.div(g, 4)
    h = lax.rem(g, 4)

    def z_peer(k):
        return lax.rem(r + k, NR)

    def c_peer(k):
        return lax.rem(me + k, NQ)

    def q_peer(k):
        return lax.rem(h + k, 4)

    barrier = pltpu.get_barrier_semaphore()

    def greet_z(k, _):
        pl.semaphore_signal(barrier, inc=1, device_id=(z_peer(k), g), device_id_type=MESH)
        return 0

    def greet_c(k, _):
        pl.semaphore_signal(barrier, inc=1, device_id=(r, c_peer(k) * 4 + h), device_id_type=MESH)
        return 0

    def greet_q(k, _):
        pl.semaphore_signal(barrier, inc=1, device_id=(r, me * 4 + q_peer(k)), device_id_type=MESH)
        return 0

    lax.fori_loop(1, NR, greet_z, 0)
    lax.fori_loop(1, NQ, greet_c, 0)
    lax.fori_loop(1, 4, greet_q, 0)

    def z_send(src, dst, sem_r, sem_s, n=BPS):
        def go(i, _):
            k = NR // 2 + lax.div(i + 1, 2) * (1 - 2 * lax.rem(i, 2))
            d = z_peer(k)
            pltpu.make_async_remote_copy(
                src_ref=src.at[pl.ds(d * n, n)], dst_ref=dst.at[pl.ds(r * n, n)],
                send_sem=sem_s, recv_sem=sem_r, device_id=(d, g), device_id_type=MESH,
            ).start()
            return 0

        lax.fori_loop(0, NR - 1, go, 0)

    def z_wait(src, dst, sem_r, sem_s, n=BPS):
        n = (NR - 1) * n
        c = pltpu.make_async_remote_copy(
            src_ref=src.at[pl.ds(0, n)], dst_ref=dst.at[pl.ds(0, n)],
            send_sem=sem_s, recv_sem=sem_r, device_id=(z_peer(1), g), device_id_type=MESH,
        )
        return c

    handler = me < ND

    def other_handlers(act):
        @pl.when(handler)
        def _():
            act(ND - 1)

        @pl.when(jnp.logical_not(handler))
        def _():
            act(ND)

    def c_send(src, dst, sem_r, sem_s, only=NQ):
        def go(i, _):
            m = c_peer(NQ // 2 + lax.div(i + 1, 2) * (1 - 2 * lax.rem(i, 2)))

            def start():
                pltpu.make_async_remote_copy(
                    src_ref=src.at[m], dst_ref=dst.at[me],
                    send_sem=sem_s, recv_sem=sem_r, device_id=(r, m * 4 + h), device_id_type=MESH,
                ).start()

            if only < NQ:
                pl.when(m < only)(start)
            else:
                start()
            return 0

        lax.fori_loop(0, NQ - 1, go, 0)

    def c_wait(src, dst, sem_r, sem_s, n=NQ - 1):
        return pltpu.make_async_remote_copy(
            src_ref=src.at[pl.ds(0, n)], dst_ref=dst.at[pl.ds(0, n)],
            send_sem=sem_s, recv_sem=sem_r, device_id=(r, c_peer(1) * 4 + h), device_id_type=MESH,
        )

    def q_send(buf, sem_r, sem_s):
        def go(k, _):
            o = q_peer(k)
            pltpu.make_async_remote_copy(
                src_ref=buf.at[h], dst_ref=buf.at[h],
                send_sem=sem_s, recv_sem=sem_r, device_id=(r, me * 4 + o), device_id_type=MESH,
            ).start()
            return 0

        lax.fori_loop(1, 4, go, 0)

    def q_wait(buf, sem_r, sem_s):
        return pltpu.make_async_remote_copy(
            src_ref=buf.at[pl.ds(0, 3)], dst_ref=buf.at[pl.ds(0, 3)],
            send_sem=sem_s, recv_sem=sem_r, device_id=(r, me * 4 + q_peer(1)), device_id_type=MESH,
        )

    zero = jnp.zeros((8, FB), jnp.float32)

    target = target_ref[...]
    member = jnp.where(iota((16, FD), 0) == target, 1.0, 0.0)
    parts = [member[:, i * FB : (i + 1) * FB] for i in range(FD // FB)]
    stacked = jnp.concatenate(parts, axis=0).astype(jnp.bfloat16)
    lanes = iota((FB, 2 * FB), 1)
    summing = jnp.where((iota((FB, 2 * FB), 0) < lanes) | (lanes >= FB), 1.0, 0.0).astype(jnp.bfloat16)
    sums = jnp.dot(stacked, summing, preferred_element_type=jnp.float32)
    count = jnp.zeros((16, FB), jnp.float32)
    ranks = []
    for i, part in enumerate(parts):
        prefix = sums[16 * i : 16 * i + 16, :FB] + count
        ranks.append(jnp.sum(part * prefix, axis=0, keepdims=True))
        count = count + sums[16 * i : 16 * i + 16, FB:]
    rank = jnp.concatenate(ranks, axis=1).astype(jnp.int32)
    hi = target * BPS + rank // FB
    oh_lo[...] = jnp.where(iota((FB, FD), 0) == rank % FB, 1.0, 0.0).astype(jnp.bfloat16)

    for c in range(NC):
        x = x_ref[pl.ds(8 * c, 8), :]
        big = x.astype(jnp.bfloat16)
        small = (x - big.astype(jnp.float32)).astype(jnp.bfloat16)
        both = jnp.concatenate([big, small], axis=0)
        for b in range(NBLK):
            keep = jnp.where(hi == b, 1.0, 0.0).astype(jnp.bfloat16)
            masked[pl.ds(16 * b, 16), :] = both * keep
        placed = lax.dot_general(
            masked[...], oh_lo[...], (((1,), (1,)), ((), ())), preferred_element_type=jnp.float32
        ).reshape(NBLK, 16, FB)
        zout[c][pl.ds(0, NBLK)] = placed[:, :8] + placed[:, 8:]
        zout[c][NBLK] = zero
        if c == 0:
            pl.semaphore_wait(barrier, (NR - 1) + (NQ - 1) + 3)
        z_send(zout[c], zin[c], sr_z.at[c], ss.at[12 + c])
        zin[c][pl.ds(r * BPS, BPS)] = zout[c][pl.ds(r * BPS, BPS)]
        if c == 0:
            blocks = (count.astype(jnp.int32) + (FB - 1)) // FB
            below = jnp.where(iota((16, 16), 1) < iota((16, 16), 0), 1.0, 0.0).astype(jnp.bfloat16)
            start = jnp.dot(
                below, blocks.astype(jnp.float32).astype(jnp.bfloat16), preferred_element_type=jnp.float32
            )
            base = [jnp.sum(part * start, axis=0, keepdims=True) for part in parts]
            hip_ref[...] = jnp.concatenate(base, axis=1).astype(jnp.int32) + rank // FB
            rows = pair_rows(pairs_ref[0:1, :], pairs_ref[1:2, :], owner_ref[...])
            rows = rows + block_rows(start.astype(jnp.int32), blocks)
            bounds = [NBLK - 1, NT - 1, 1, NT, NG - 1, NBLK, NT - 1]
            rows = [jnp.clip(row, 0, high) for row, high in zip(rows, bounds)]
            tabv[...] = jnp.concatenate(rows + [jnp.zeros((1, FB), jnp.int32)], axis=0)
            tab_copy = pltpu.make_async_copy(tabv, tab, tab_sem)
            tab_copy.start()
    tab_copy.wait()

    for t in range(PACKED):
        for c in range(NC):
            gdo[t // 2, t % 2, c] = zout[c][tab[T_IDX, t]]
    c_send(gdo, gdi, sr_gd, ss.at[1], only=ND)
    mdi[NQ - 1, 1] = zero

    def block_of(ref, u):
        return ref[:, u].reshape(NQ * NC * 8, FB)

    def gram(a, b):
        return lax.dot_general(a, b, (((0,), (0,)), ((), ())), precision=HIGHEST, preferred_element_type=jnp.float32)

    for c in range(NC):
        if c == NC - 1:


            @pl.when(handler)
            def _():
                gdi[me] = gdo[me]
                c_wait(gdo, gdi, sr_gd, ss.at[1]).wait_recv()
                for u in range(2):
                    xu = block_of(gdi, u)
                    qd[h, u] = gram(xu, xu)
                q_send(qd, sr_qd, ss.at[2])

        z_wait(zout[c], zin[c], sr_z.at[c], ss.at[12 + c]).wait_recv()
        for k in range(NQ):
            for u in range(2):
                goo[c][k, u] = zin[c][tab[T_UNIT, u * NQ + k]]
        c_send(goo[c], goi[c], sr_go.at[c], ss.at[15 + c])
        goi[c][me] = goo[c][me]

    @pl.when(handler)
    def _():
        q_wait(qd, sr_qd, ss.at[2]).wait_recv()
        eye = jnp.where(iota((FB, FB), 0) == iota((FB, FB), 1), 1.0, 0.0)
        for u in range(2):
            m = qd[0, u] + qd[1, u] + qd[2, u] + qd[3, u]
            mdo[:, u] = m.reshape(NQ, 8, FB)
            shift = m * (1.0 / COEFFICIENT_SIZE) - eye
            change = jnp.dot(block_of(gdi, u), shift, precision=HIGHEST, preferred_element_type=jnp.float32)
            rdo[:, u] = change.reshape(NQ, NC, 8, FB)
        c_send(mdo, mdi, sr_md, ss.at[4])
        mdi[me] = mdo[me]

    total = None
    for c in range(NC):
        c_wait(goo[c], goi[c], sr_go.at[c], ss.at[15 + c]).wait_recv()
        part = gram(goi[c][:, 0].reshape(NQ * 8, FB), goi[c][:, 1].reshape(NQ * 8, FB))
        total = part if total is None else total + part
    qo[h] = total
    q_send(qo, sr_qo, ss.at[5])

    other_handlers(lambda n: c_wait(mdo, mdi, sr_md, ss.at[4], n).wait_recv())
    for d in range(NR):
        t = tab[T_INV, d * BPS + h]
        mzo[d] = mdi[lax.div(t, 2), lax.rem(t, 2)]
    z_send(mzo, mq.at[h], sr_mz, ss.at[6], 1)
    mq[h, r] = mzo[r]

    q_wait(qo, sr_qo, ss.at[5]).wait_recv()
    m = qo[0] + qo[1] + qo[2] + qo[3]
    mko[...] = m.reshape(NQ, 8, FB)
    m = m * (1.0 / COEFFICIENT_SIZE)
    for c in range(NC):
        lc, rc = goi[c][:, 0].reshape(NQ * 8, FB), goi[c][:, 1].reshape(NQ * 8, FB)
        to_left = lax.dot_general(
            rc, m, (((1,), (1,)), ((), ())), precision=HIGHEST, preferred_element_type=jnp.float32
        )
        roo[c][:, 0] = to_left.reshape(NQ, 8, FB)
        roo[c][:, 1] = jnp.dot(lc, m, precision=HIGHEST, preferred_element_type=jnp.float32).reshape(NQ, 8, FB)
        c_send(roo[c], roi[c], sr_ro.at[c], ss.at[18 + c])
        roi[c][me] = roo[c][me]

    c_send(mko, moi, sr_mo, ss.at[8])
    moi[me] = mko[me]

    @pl.when(handler)
    def _():
        c_send(rdo, rdi, sr_rd, ss.at[9])
        rdi[me] = rdo[me]

    seg[NT] = zero
    for c in range(NC):
        c_wait(roo[c], roi[c], sr_ro.at[c], ss.at[18 + c]).wait_recv()
        total = zero
        for i in range(NT):
            p = tab[T_PERM, i]
            total = roi[c][lax.rem(p, NQ), lax.div(p, NQ)] + total * tab[T_SAME, i].astype(jnp.float32)
            seg[i] = total
        for b in range(NBLK):
            zro[c][b] = seg[tab[T_LAST, b]]
        z_send(zro[c], zri[c], sr_zr.at[c], ss.at[21 + c])
        zri[c][pl.ds(r * BPS, BPS)] = zro[c][pl.ds(r * BPS, BPS)]
        zri[c][NBLK] = zero

    z_wait(mzo, mq.at[h], sr_mz, ss.at[6], 1).wait_recv()
    q_send(mq, sr_mq, ss.at[0])
    c_wait(mko, moi, sr_mo, ss.at[8]).wait_recv()
    q_wait(mq, sr_mq, ss.at[0]).wait_recv()
    for b in range(NBLK):
        mall[b] = mq[b % BPS, b // BPS]
    mall[pl.ds(NBLK, NQ)] = moi[...]
    for i in range(NQ):
        mfo[i] = mall[tab[T_POS, 4 * i + h]]
    c_send(mfo, mfi, sr_mf, ss.at[11])
    mfi[me] = mfo[me]

    other_handlers(lambda n: c_wait(rdo, rdi, sr_rd, ss.at[9], n).wait_recv())
    hip = hip_ref[...]
    for c in range(NC):
        z_wait(zro[c], zri[c], sr_zr.at[c], ss.at[21 + c]).wait_recv()
        for t in range(PACKED):
            u = gdo[t // 2, t % 2, c] - 0.5 * (rdi[t // 2, t % 2, c] + zri[c][tab[T_IDX, t]])
            big = u.astype(jnp.bfloat16)
            small = (u - big.astype(jnp.float32)).astype(jnp.bfloat16)
            upd[pl.ds(16 * t, 16), :] = jnp.concatenate([big, small], axis=0)
        picked[...] = jnp.dot(upd[...], oh_lo[...], preferred_element_type=jnp.float32)
        for part, ref in enumerate((big_ref, small_ref)):
            total = jnp.zeros((8, FD), jnp.float32)
            for t in range(PACKED):
                total = total + jnp.where(hip == t, picked[pl.ds(16 * t + 8 * part, 8), :], 0.0)
            ref[pl.ds(8 * c, 8), :] = total

    c_wait(mfo, mfi, sr_mf, ss.at[11]).wait_recv()
    margin_ref[...] = mfi[...].reshape(FB, FB)

    for c in range(NC):
        z_wait(zout[c], zin[c], sr_z.at[c], ss.at[12 + c]).wait_send()
        c_wait(goo[c], goi[c], sr_go.at[c], ss.at[15 + c]).wait_send()
        c_wait(roo[c], roi[c], sr_ro.at[c], ss.at[18 + c]).wait_send()
        z_wait(zro[c], zri[c], sr_zr.at[c], ss.at[21 + c]).wait_send()
    other_handlers(lambda n: c_wait(gdo, gdi, sr_gd, ss.at[1], n).wait_send())

    @pl.when(handler)
    def _():
        q_wait(qd, sr_qd, ss.at[2]).wait_send()
        c_wait(mdo, mdi, sr_md, ss.at[4]).wait_send()
        c_wait(rdo, rdi, sr_rd, ss.at[9]).wait_send()

    q_wait(qo, sr_qo, ss.at[5]).wait_send()
    z_wait(mzo, mq.at[h], sr_mz, ss.at[6], 1).wait_send()
    c_wait(mko, moi, sr_mo, ss.at[8]).wait_send()
    q_wait(mq, sr_mq, ss.at[0]).wait_send()
    c_wait(mfo, mfi, sr_mf, ss.at[11]).wait_send()


def body(coeffs, region_of, block_pairs, block_owner):
    f32, bf16 = jnp.float32, jnp.bfloat16
    v = pltpu.VMEM
    tile = (8, FB)
    dma = pltpu.SemaphoreType.DMA
    vm = pl.BlockSpec(memory_space=pltpu.VMEM)
    z = [v((NBLK + 1, *tile), f32) for _ in range(NC)]
    pr = [v((NQ, 2, *tile), f32) for _ in range(NC)]
    un = v((NQ, 2, NC, *tile), f32)
    big, small, margin = pl.pallas_call(
        kernel,
        out_shape=(
            jax.ShapeDtypeStruct((ROWS, FD), f32),
            jax.ShapeDtypeStruct((ROWS, FD), f32),
            jax.ShapeDtypeStruct((FB, FB), f32),
        ),
        in_specs=[vm, vm, vm, vm],
        out_specs=(vm, vm, vm),
        scratch_shapes=[
            v((8, FB), jnp.int32), pltpu.SMEM((8, FB), jnp.int32), v((1, FD), jnp.int32), dma,
            v((FB, FD), bf16), v((NBLK * 16, FD), bf16), z, z, un, un, pr, pr,
            v((4, 2, FB, FB), f32), v((4, FB, FB), f32), un, un, pr, pr, v((NT + 1, *tile), f32), z, z,
            v((NQ, 2, *tile), f32), v((NQ, 2, *tile), f32), v((NR, *tile), f32), v((4, NR, *tile), f32),
            v((NQ, *tile), f32), v((NQ, *tile), f32), v((NG, *tile), f32), v((NQ, *tile), f32), v((NQ, *tile), f32),
            v((PACKED * 16, FB), bf16), v((PACKED * 16, FD), f32),
            dma((24,)), dma((NC,)), dma, dma((NC,)), dma, dma, dma, dma((NC,)), dma((NC,)), dma, dma, dma, dma, dma,
        ],
        compiler_params=pltpu.CompilerParams(collective_id=0, has_side_effects=True, vmem_limit_bytes=56 * 2**20),
    )(coeffs, region_of.reshape(1, FD), block_pairs[0].T, block_owner)
    return big + small, (margin * (1.0 / COEFFICIENT_SIZE))[None, None]


def solution(mesh):
    placed = (P("group", "region"), P("region", None), P("region", None, None), P("region", None))
    return jax.shard_map(
        body,
        mesh=mesh,
        in_specs=placed,
        out_specs=(P("group", "region"), P("region", "group", None, None)),
        check_vma=False,
    )
```

```python
import functools

import jax
import jax.numpy as jnp
from jax import lax
from jax.experimental import pallas as pl
from jax.experimental.pallas import tpu as pltpu
from jax.sharding import PartitionSpec as P

COEFFICIENT_SIZE = 1536
FB = 128
BPS = 4
FD = 2048
NR = 12
NG = 64
NBLK = NR * BPS
NQ = NG // 4
ROWS = 24
NC = ROWS // 8
NT = 2 * NQ
PACKED = 28
ND = PACKED // 2
MESH = pl.DeviceIdType.MESH
HIGHEST = lax.Precision.HIGHEST

T_UNIT, T_PERM, T_SAME, T_LAST, T_POS, T_IDX, T_INV = range(7)


def iota(shape, axis):
    return lax.broadcasted_iota(jnp.int32, shape, axis)


def column(row, n):
    shape = (n, row.shape[1])
    spread = jnp.where(iota(shape, 0) == iota(shape, 1), row, 0)
    return jnp.sum(spread.astype(jnp.float32), axis=1, keepdims=True).astype(jnp.int32)


def pair_rows(left_row, right_row, owner_row):
    left, right = column(left_row, NG), column(right_row, NG)
    lane = iota((NG, FB), 1)
    off = (left != right).astype(jnp.int32)
    off_row = (left_row != right_row).astype(jnp.int32)
    before = jnp.where(iota((NG, NG), 1) < iota((NG, NG), 0), off_row, 0)
    off_rank = jnp.sum(before.astype(jnp.float32), axis=1, keepdims=True).astype(jnp.int32)
    hit = (lane < NT) & (off == 1) & (off_rank == lane % NQ)
    unit = jnp.sum(jnp.where(hit, jnp.where(lane < NQ, left, right), 0), axis=0, keepdims=True)
    u, r = iota((NT, FB), 0), iota((NT, FB), 1)
    dest = column(unit, NT)
    key_row = unit * NT + iota((1, FB), 1)
    key = dest * NT + iota((NT, 1), 0)
    smaller = jnp.where((r < NT) & (key_row < key), 1.0, 0.0)
    rank = jnp.sum(smaller, axis=1, keepdims=True).astype(jnp.int32)
    perm = jnp.sum(jnp.where(rank == r, u, 0), axis=0, keepdims=True)
    here = jnp.sum(jnp.where(rank == r, dest, 0), axis=0, keepdims=True)
    previous = jnp.sum(jnp.where(rank == r - 1, dest, 0), axis=0, keepdims=True)
    same = jnp.where((here == previous) & (iota((1, FB), 1) > 0), 1, 0)
    last = jnp.max(jnp.where(dest == r, rank, -1), axis=0, keepdims=True)
    last = jnp.where(last < 0, NT, last)
    piece = jnp.where(off == 1, NBLK + off_rank, left)
    pos = jnp.sum(jnp.where(column(owner_row, NG) == lane, piece, 0), axis=0, keepdims=True)
    return [unit, perm, same, last, pos]


def block_rows(start, blocks):
    d, t = iota((16, FB), 0), iota((16, FB), 1)
    inside = (t >= start) & (t < start + blocks)
    idx = jnp.sum(jnp.where(inside, d * BPS + t - start + 1, 0), axis=0, keepdims=True) - 1
    idx = jnp.where(idx < 0, NBLK, idx)
    mine = (t // BPS == d) & (t % BPS < blocks)
    inv = jnp.sum(jnp.where(mine, start + t % BPS + 1, 0), axis=0, keepdims=True) - 1
    inv = jnp.where(inv < 0, NT - 1, inv)
    return [idx, inv]


def kernel(
    x_ref, target_ref, pairs_ref, owner_ref, big_ref, small_ref, margin_ref,
    tabv, tab, hip_ref, tab_sem, oh_lo, masked, zout, zin, gdo, gdi, goo, goi, qd, qo, rdo, rdi, roo, roi, seg, zro, zri,
    mdo, mdi, mzo, mq, mko, moi, mall, mfo, mfi, upd, picked,
    ss, sr_z, sr_gd, sr_go, sr_qd, sr_qo, sr_rd, sr_ro, sr_zr, sr_md, sr_mz, sr_mq, sr_mo, sr_mf,
):
    r = lax.axis_index("region")
    g = lax.axis_index("group")
    me = lax.div(g, 4)
    h = lax.rem(g, 4)

    def z_peer(k):
        return lax.rem(r + k, NR)

    def c_peer(k):
        return lax.rem(me + k, NQ)

    def q_peer(k):
        return lax.rem(h + k, 4)

    barrier = pltpu.get_barrier_semaphore()

    def greet_z(k, _):
        pl.semaphore_signal(barrier, inc=1, device_id=(z_peer(k), g), device_id_type=MESH)
        return 0

    def greet_c(k, _):
        pl.semaphore_signal(barrier, inc=1, device_id=(r, c_peer(k) * 4 + h), device_id_type=MESH)
        return 0

    def greet_q(k, _):
        pl.semaphore_signal(barrier, inc=1, device_id=(r, me * 4 + q_peer(k)), device_id_type=MESH)
        return 0

    lax.fori_loop(1, NR, greet_z, 0)
    lax.fori_loop(1, NQ, greet_c, 0)
    lax.fori_loop(1, 4, greet_q, 0)

    def z_send(src, dst, sem_r, sem_s, n=BPS):
        def go(i, _):
            k = NR // 2 + lax.div(i + 1, 2) * (1 - 2 * lax.rem(i, 2))
            d = z_peer(k)
            pltpu.make_async_remote_copy(
                src_ref=src.at[pl.ds(d * n, n)], dst_ref=dst.at[pl.ds(r * n, n)],
                send_sem=sem_s, recv_sem=sem_r, device_id=(d, g), device_id_type=MESH,
            ).start()
            return 0

        lax.fori_loop(0, NR - 1, go, 0)

    def z_wait(src, dst, sem_r, sem_s, n=BPS):
        n = (NR - 1) * n
        c = pltpu.make_async_remote_copy(
            src_ref=src.at[pl.ds(0, n)], dst_ref=dst.at[pl.ds(0, n)],
            send_sem=sem_s, recv_sem=sem_r, device_id=(z_peer(1), g), device_id_type=MESH,
        )
        return c

    handler = me < ND

    def other_handlers(act):
        @pl.when(handler)
        def _():
            act(ND - 1)

        @pl.when(jnp.logical_not(handler))
        def _():
            act(ND)

    def c_send(src, dst, sem_r, sem_s, only=NQ):
        def go(i, _):
            m = c_peer(NQ // 2 + lax.div(i + 1, 2) * (1 - 2 * lax.rem(i, 2)))

            def start():
                pltpu.make_async_remote_copy(
                    src_ref=src.at[m], dst_ref=dst.at[me],
                    send_sem=sem_s, recv_sem=sem_r, device_id=(r, m * 4 + h), device_id_type=MESH,
                ).start()

            if only < NQ:
                pl.when(m < only)(start)
            else:
                start()
            return 0

        lax.fori_loop(0, NQ - 1, go, 0)

    def c_wait(src, dst, sem_r, sem_s, n=NQ - 1):
        return pltpu.make_async_remote_copy(
            src_ref=src.at[pl.ds(0, n)], dst_ref=dst.at[pl.ds(0, n)],
            send_sem=sem_s, recv_sem=sem_r, device_id=(r, c_peer(1) * 4 + h), device_id_type=MESH,
        )

    def q_send(buf, sem_r, sem_s):
        def go(k, _):
            o = q_peer(k)
            pltpu.make_async_remote_copy(
                src_ref=buf.at[h], dst_ref=buf.at[h],
                send_sem=sem_s, recv_sem=sem_r, device_id=(r, me * 4 + o), device_id_type=MESH,
            ).start()
            return 0

        lax.fori_loop(1, 4, go, 0)

    def q_wait(buf, sem_r, sem_s):
        return pltpu.make_async_remote_copy(
            src_ref=buf.at[pl.ds(0, 3)], dst_ref=buf.at[pl.ds(0, 3)],
            send_sem=sem_s, recv_sem=sem_r, device_id=(r, me * 4 + q_peer(1)), device_id_type=MESH,
        )

    zero = jnp.zeros((8, FB), jnp.float32)

    target = target_ref[...]
    member = jnp.where(iota((16, FD), 0) == target, 1.0, 0.0)
    parts = [member[:, i * FB : (i + 1) * FB] for i in range(FD // FB)]
    stacked = jnp.concatenate(parts, axis=0).astype(jnp.bfloat16)
    lanes = iota((FB, 2 * FB), 1)
    summing = jnp.where((iota((FB, 2 * FB), 0) < lanes) | (lanes >= FB), 1.0, 0.0).astype(jnp.bfloat16)
    sums = jnp.dot(stacked, summing, preferred_element_type=jnp.float32)
    count = jnp.zeros((16, FB), jnp.float32)
    ranks = []
    for i, part in enumerate(parts):
        prefix = sums[16 * i : 16 * i + 16, :FB] + count
        ranks.append(jnp.sum(part * prefix, axis=0, keepdims=True))
        count = count + sums[16 * i : 16 * i + 16, FB:]
    rank = jnp.concatenate(ranks, axis=1).astype(jnp.int32)
    hi = target * BPS + rank // FB
    oh_lo[...] = jnp.where(iota((FB, FD), 0) == rank % FB, 1.0, 0.0).astype(jnp.bfloat16)

    for c in range(NC):
        x = x_ref[pl.ds(8 * c, 8), :]
        big = x.astype(jnp.bfloat16)
        small = (x - big.astype(jnp.float32)).astype(jnp.bfloat16)
        both = jnp.concatenate([big, small], axis=0)
        for b in range(NBLK):
            keep = jnp.where(hi == b, 1.0, 0.0).astype(jnp.bfloat16)
            masked[pl.ds(16 * b, 16), :] = both * keep
        placed = lax.dot_general(
            masked[...], oh_lo[...], (((1,), (1,)), ((), ())), preferred_element_type=jnp.float32
        ).reshape(NBLK, 16, FB)
        zout[c][pl.ds(0, NBLK)] = placed[:, :8] + placed[:, 8:]
        zout[c][NBLK] = zero
        if c == 0:
            pl.semaphore_wait(barrier, (NR - 1) + (NQ - 1) + 3)
        z_send(zout[c], zin[c], sr_z.at[c], ss.at[12 + c])
        zin[c][pl.ds(r * BPS, BPS)] = zout[c][pl.ds(r * BPS, BPS)]
        if c == 0:
            blocks = (count.astype(jnp.int32) + (FB - 1)) // FB
            below = jnp.where(iota((16, 16), 1) < iota((16, 16), 0), 1.0, 0.0).astype(jnp.bfloat16)
            start = jnp.dot(
                below, blocks.astype(jnp.float32).astype(jnp.bfloat16), preferred_element_type=jnp.float32
            )
            base = [jnp.sum(part * start, axis=0, keepdims=True) for part in parts]
            hip_ref[...] = jnp.concatenate(base, axis=1).astype(jnp.int32) + rank // FB
            rows = pair_rows(pairs_ref[0:1, :], pairs_ref[1:2, :], owner_ref[...])
            rows = rows + block_rows(start.astype(jnp.int32), blocks)
            bounds = [NBLK - 1, NT - 1, 1, NT, NG - 1, NBLK, NT - 1]
            rows = [jnp.clip(row, 0, high) for row, high in zip(rows, bounds)]
            tabv[...] = jnp.concatenate(rows + [jnp.zeros((1, FB), jnp.int32)], axis=0)
            tab_copy = pltpu.make_async_copy(tabv, tab, tab_sem)
            tab_copy.start()
    tab_copy.wait()

    for t in range(PACKED):
        for c in range(NC):
            gdo[t // 2, t % 2, c] = zout[c][tab[T_IDX, t]]
    c_send(gdo, gdi, sr_gd, ss.at[1], only=ND)
    mdi[NQ - 1, 1] = zero

    def block_of(ref, u):
        return ref[:, u].reshape(NQ * NC * 8, FB)

    def gram(a, b):
        return lax.dot_general(a, b, (((0,), (0,)), ((), ())), precision=HIGHEST, preferred_element_type=jnp.float32)

    for c in range(NC):
        if c == NC - 1:


            @pl.when(handler)
            def _():
                gdi[me] = gdo[me]
                c_wait(gdo, gdi, sr_gd, ss.at[1]).wait_recv()
                for u in range(2):
                    xu = block_of(gdi, u)
                    qd[h, u] = gram(xu, xu)
                q_send(qd, sr_qd, ss.at[2])

        z_wait(zout[c], zin[c], sr_z.at[c], ss.at[12 + c]).wait_recv()
        for k in range(NQ):
            for u in range(2):
                goo[c][k, u] = zin[c][tab[T_UNIT, u * NQ + k]]
        c_send(goo[c], goi[c], sr_go.at[c], ss.at[15 + c])
        goi[c][me] = goo[c][me]

    total = None
    for c in range(NC):
        c_wait(goo[c], goi[c], sr_go.at[c], ss.at[15 + c]).wait_recv()
        part = gram(goi[c][:, 0].reshape(NQ * 8, FB), goi[c][:, 1].reshape(NQ * 8, FB))
        total = part if total is None else total + part
    qo[h] = total
    q_send(qo, sr_qo, ss.at[5])

    @pl.when(handler)
    def _():
        q_wait(qd, sr_qd, ss.at[2]).wait_recv()
        eye = jnp.where(iota((FB, FB), 0) == iota((FB, FB), 1), 1.0, 0.0)
        for u in range(2):
            m = qd[0, u] + qd[1, u] + qd[2, u] + qd[3, u]
            mdo[:, u] = m.reshape(NQ, 8, FB)
            shift = m * (1.0 / COEFFICIENT_SIZE) - eye
            change = jnp.dot(block_of(gdi, u), shift, precision=HIGHEST, preferred_element_type=jnp.float32)
            rdo[:, u] = change.reshape(NQ, NC, 8, FB)
        c_send(mdo, mdi, sr_md, ss.at[4])
        mdi[me] = mdo[me]


    q_wait(qo, sr_qo, ss.at[5]).wait_recv()
    m = qo[0] + qo[1] + qo[2] + qo[3]
    mko[...] = m.reshape(NQ, 8, FB)
    m = m * (1.0 / COEFFICIENT_SIZE)
    for c in range(NC):
        lc, rc = goi[c][:, 0].reshape(NQ * 8, FB), goi[c][:, 1].reshape(NQ * 8, FB)
        to_left = lax.dot_general(
            rc, m, (((1,), (1,)), ((), ())), precision=HIGHEST, preferred_element_type=jnp.float32
        )
        roo[c][:, 0] = to_left.reshape(NQ, 8, FB)
        roo[c][:, 1] = jnp.dot(lc, m, precision=HIGHEST, preferred_element_type=jnp.float32).reshape(NQ, 8, FB)
        c_send(roo[c], roi[c], sr_ro.at[c], ss.at[18 + c])
        roi[c][me] = roo[c][me]

    c_send(mko, moi, sr_mo, ss.at[8])
    moi[me] = mko[me]

    @pl.when(handler)
    def _():
        c_send(rdo, rdi, sr_rd, ss.at[9])
        rdi[me] = rdo[me]

    other_handlers(lambda n: c_wait(mdo, mdi, sr_md, ss.at[4], n).wait_recv())
    for d in range(NR):
        t = tab[T_INV, d * BPS + h]
        mzo[d] = mdi[lax.div(t, 2), lax.rem(t, 2)]
    z_send(mzo, mq.at[h], sr_mz, ss.at[6], 1)
    mq[h, r] = mzo[r]

    seg[NT] = zero
    for c in range(NC):
        c_wait(roo[c], roi[c], sr_ro.at[c], ss.at[18 + c]).wait_recv()
        total = zero
        for i in range(NT):
            p = tab[T_PERM, i]
            total = roi[c][lax.rem(p, NQ), lax.div(p, NQ)] + total * tab[T_SAME, i].astype(jnp.float32)
            seg[i] = total
        for b in range(NBLK):
            zro[c][b] = seg[tab[T_LAST, b]]
        z_send(zro[c], zri[c], sr_zr.at[c], ss.at[21 + c])
        zri[c][pl.ds(r * BPS, BPS)] = zro[c][pl.ds(r * BPS, BPS)]
        zri[c][NBLK] = zero

    z_wait(mzo, mq.at[h], sr_mz, ss.at[6], 1).wait_recv()
    q_send(mq, sr_mq, ss.at[0])
    c_wait(mko, moi, sr_mo, ss.at[8]).wait_recv()
    q_wait(mq, sr_mq, ss.at[0]).wait_recv()
    for b in range(NBLK):
        mall[b] = mq[b % BPS, b // BPS]
    mall[pl.ds(NBLK, NQ)] = moi[...]
    for i in range(NQ):
        mfo[i] = mall[tab[T_POS, 4 * i + h]]
    c_send(mfo, mfi, sr_mf, ss.at[11])
    mfi[me] = mfo[me]

    other_handlers(lambda n: c_wait(rdo, rdi, sr_rd, ss.at[9], n).wait_recv())
    hip = hip_ref[...]
    for c in range(NC):
        z_wait(zro[c], zri[c], sr_zr.at[c], ss.at[21 + c]).wait_recv()
        for t in range(PACKED):
            u = gdo[t // 2, t % 2, c] - 0.5 * (rdi[t // 2, t % 2, c] + zri[c][tab[T_IDX, t]])
            big = u.astype(jnp.bfloat16)
            small = (u - big.astype(jnp.float32)).astype(jnp.bfloat16)
            upd[pl.ds(16 * t, 16), :] = jnp.concatenate([big, small], axis=0)
        picked[...] = jnp.dot(upd[...], oh_lo[...], preferred_element_type=jnp.float32)
        for part, ref in enumerate((big_ref, small_ref)):
            total = jnp.zeros((8, FD), jnp.float32)
            for t in range(PACKED):
                total = total + jnp.where(hip == t, picked[pl.ds(16 * t + 8 * part, 8), :], 0.0)
            ref[pl.ds(8 * c, 8), :] = total

    c_wait(mfo, mfi, sr_mf, ss.at[11]).wait_recv()
    margin_ref[...] = mfi[...].reshape(FB, FB)

    for c in range(NC):
        z_wait(zout[c], zin[c], sr_z.at[c], ss.at[12 + c]).wait_send()
        c_wait(goo[c], goi[c], sr_go.at[c], ss.at[15 + c]).wait_send()
        c_wait(roo[c], roi[c], sr_ro.at[c], ss.at[18 + c]).wait_send()
        z_wait(zro[c], zri[c], sr_zr.at[c], ss.at[21 + c]).wait_send()
    other_handlers(lambda n: c_wait(gdo, gdi, sr_gd, ss.at[1], n).wait_send())

    @pl.when(handler)
    def _():
        q_wait(qd, sr_qd, ss.at[2]).wait_send()
        c_wait(mdo, mdi, sr_md, ss.at[4]).wait_send()
        c_wait(rdo, rdi, sr_rd, ss.at[9]).wait_send()

    q_wait(qo, sr_qo, ss.at[5]).wait_send()
    z_wait(mzo, mq.at[h], sr_mz, ss.at[6], 1).wait_send()
    c_wait(mko, moi, sr_mo, ss.at[8]).wait_send()
    q_wait(mq, sr_mq, ss.at[0]).wait_send()
    c_wait(mfo, mfi, sr_mf, ss.at[11]).wait_send()


def body(coeffs, region_of, block_pairs, block_owner):
    f32, bf16 = jnp.float32, jnp.bfloat16
    v = pltpu.VMEM
    tile = (8, FB)
    dma = pltpu.SemaphoreType.DMA
    vm = pl.BlockSpec(memory_space=pltpu.VMEM)
    z = [v((NBLK + 1, *tile), f32) for _ in range(NC)]
    pr = [v((NQ, 2, *tile), f32) for _ in range(NC)]
    un = v((NQ, 2, NC, *tile), f32)
    big, small, margin = pl.pallas_call(
        kernel,
        out_shape=(
            jax.ShapeDtypeStruct((ROWS, FD), f32),
            jax.ShapeDtypeStruct((ROWS, FD), f32),
            jax.ShapeDtypeStruct((FB, FB), f32),
        ),
        in_specs=[vm, vm, vm, vm],
        out_specs=(vm, vm, vm),
        scratch_shapes=[
            v((8, FB), jnp.int32), pltpu.SMEM((8, FB), jnp.int32), v((1, FD), jnp.int32), dma,
            v((FB, FD), bf16), v((NBLK * 16, FD), bf16), z, z, un, un, pr, pr,
            v((4, 2, FB, FB), f32), v((4, FB, FB), f32), un, un, pr, pr, v((NT + 1, *tile), f32), z, z,
            v((NQ, 2, *tile), f32), v((NQ, 2, *tile), f32), v((NR, *tile), f32), v((4, NR, *tile), f32),
            v((NQ, *tile), f32), v((NQ, *tile), f32), v((NG, *tile), f32), v((NQ, *tile), f32), v((NQ, *tile), f32),
            v((PACKED * 16, FB), bf16), v((PACKED * 16, FD), f32),
            dma((24,)), dma((NC,)), dma, dma((NC,)), dma, dma, dma, dma((NC,)), dma((NC,)), dma, dma, dma, dma, dma,
        ],
        compiler_params=pltpu.CompilerParams(collective_id=0, has_side_effects=True, vmem_limit_bytes=56 * 2**20),
    )(coeffs, region_of.reshape(1, FD), block_pairs[0].T, block_owner)
    return big + small, (margin * (1.0 / COEFFICIENT_SIZE))[None, None]


def solution(mesh):
    placed = (P("group", "region"), P("region", None), P("region", None, None), P("region", None))
    return jax.shard_map(
        body,
        mesh=mesh,
        in_specs=placed,
        out_specs=(P("group", "region"), P("region", "group", None, None)),
        check_vma=False,
    )
```

```python
import functools

import jax
import jax.numpy as jnp
from jax import lax
from jax.experimental import pallas as pl
from jax.experimental.pallas import tpu as pltpu
from jax.sharding import PartitionSpec as P

COEFFICIENT_SIZE = 1536
FB = 128
BPS = 4
FD = 2048
NR = 12
NG = 64
NBLK = NR * BPS
NQ = NG // 4
ROWS = 24
NC = ROWS // 8
NT = 2 * NQ
PACKED = 28
ND = PACKED // 2
MESH = pl.DeviceIdType.MESH
HIGHEST = lax.Precision.HIGHEST

T_UNIT, T_PERM, T_SAME, T_LAST, T_POS, T_IDX, T_INV = range(7)


def iota(shape, axis):
    return lax.broadcasted_iota(jnp.int32, shape, axis)


def column(row, n):
    shape = (n, row.shape[1])
    spread = jnp.where(iota(shape, 0) == iota(shape, 1), row, 0)
    return jnp.sum(spread.astype(jnp.float32), axis=1, keepdims=True).astype(jnp.int32)


def pair_rows(left_row, right_row, owner_row):
    left, right = column(left_row, NG), column(right_row, NG)
    lane = iota((NG, FB), 1)
    off = (left != right).astype(jnp.int32)
    off_row = (left_row != right_row).astype(jnp.int32)
    before = jnp.where(iota((NG, NG), 1) < iota((NG, NG), 0), off_row, 0)
    off_rank = jnp.sum(before.astype(jnp.float32), axis=1, keepdims=True).astype(jnp.int32)
    hit = (lane < NT) & (off == 1) & (off_rank == lane % NQ)
    unit = jnp.sum(jnp.where(hit, jnp.where(lane < NQ, left, right), 0), axis=0, keepdims=True)
    u, r = iota((NT, FB), 0), iota((NT, FB), 1)
    dest = column(unit, NT)
    key_row = unit * NT + iota((1, FB), 1)
    key = dest * NT + iota((NT, 1), 0)
    smaller = jnp.where((r < NT) & (key_row < key), 1.0, 0.0)
    rank = jnp.sum(smaller, axis=1, keepdims=True).astype(jnp.int32)
    perm = jnp.sum(jnp.where(rank == r, u, 0), axis=0, keepdims=True)
    here = jnp.sum(jnp.where(rank == r, dest, 0), axis=0, keepdims=True)
    previous = jnp.sum(jnp.where(rank == r - 1, dest, 0), axis=0, keepdims=True)
    same = jnp.where((here == previous) & (iota((1, FB), 1) > 0), 1, 0)
    last = jnp.max(jnp.where(dest == r, rank, -1), axis=0, keepdims=True)
    last = jnp.where(last < 0, NT, last)
    piece = jnp.where(off == 1, NBLK + off_rank, left)
    pos = jnp.sum(jnp.where(column(owner_row, NG) == lane, piece, 0), axis=0, keepdims=True)
    return [unit, perm, same, last, pos]


def block_rows(start, blocks):
    d, t = iota((16, FB), 0), iota((16, FB), 1)
    inside = (t >= start) & (t < start + blocks)
    idx = jnp.sum(jnp.where(inside, d * BPS + t - start + 1, 0), axis=0, keepdims=True) - 1
    idx = jnp.where(idx < 0, NBLK, idx)
    mine = (t // BPS == d) & (t % BPS < blocks)
    inv = jnp.sum(jnp.where(mine, start + t % BPS + 1, 0), axis=0, keepdims=True) - 1
    inv = jnp.where(inv < 0, NT - 1, inv)
    return [idx, inv]


def kernel(
    x_ref, target_ref, pairs_ref, owner_ref, out_ref, margin_ref,
    tabv, tab, hip_ref, tab_sem, oh_lo, masked, zout, zin, gdo, gdi, goo, goi, qd, qo, rdo, rdi, roo, roi, seg, zro, zri,
    mdo, mdi, mzo, mq, mko, moi, mall, mfo, mfi, upd, picked,
    ss, sr_z, sr_gd, sr_go, sr_qd, sr_qo, sr_rd, sr_ro, sr_zr, sr_md, sr_mz, sr_mq, sr_mo, sr_mf,
):
    r = lax.axis_index("region")
    g = lax.axis_index("group")
    me = lax.div(g, 4)
    h = lax.rem(g, 4)

    def z_peer(k):
        return lax.rem(r + k, NR)

    def c_peer(k):
        return lax.rem(me + k, NQ)

    def q_peer(k):
        return lax.rem(h + k, 4)

    barrier = pltpu.get_barrier_semaphore()

    def greet_z(k, _):
        pl.semaphore_signal(barrier, inc=1, device_id=(z_peer(k), g), device_id_type=MESH)
        return 0

    def greet_c(k, _):
        pl.semaphore_signal(barrier, inc=1, device_id=(r, c_peer(k) * 4 + h), device_id_type=MESH)
        return 0

    def greet_q(k, _):
        pl.semaphore_signal(barrier, inc=1, device_id=(r, me * 4 + q_peer(k)), device_id_type=MESH)
        return 0

    lax.fori_loop(1, NR, greet_z, 0)
    lax.fori_loop(1, NQ, greet_c, 0)
    lax.fori_loop(1, 4, greet_q, 0)

    def z_send(src, dst, sem_r, sem_s, n=BPS):
        def go(i, _):
            k = NR // 2 + lax.div(i + 1, 2) * (1 - 2 * lax.rem(i, 2))
            d = z_peer(k)
            pltpu.make_async_remote_copy(
                src_ref=src.at[pl.ds(d * n, n)], dst_ref=dst.at[pl.ds(r * n, n)],
                send_sem=sem_s, recv_sem=sem_r, device_id=(d, g), device_id_type=MESH,
            ).start()
            return 0

        lax.fori_loop(0, NR - 1, go, 0)

    def z_wait(src, dst, sem_r, sem_s, n=BPS):
        n = (NR - 1) * n
        c = pltpu.make_async_remote_copy(
            src_ref=src.at[pl.ds(0, n)], dst_ref=dst.at[pl.ds(0, n)],
            send_sem=sem_s, recv_sem=sem_r, device_id=(z_peer(1), g), device_id_type=MESH,
        )
        return c

    handler = me < ND

    def other_handlers(act):
        @pl.when(handler)
        def _():
            act(ND - 1)

        @pl.when(jnp.logical_not(handler))
        def _():
            act(ND)

    def c_send(src, dst, sem_r, sem_s, only=NQ):
        def go(i, _):
            m = c_peer(NQ // 2 + lax.div(i + 1, 2) * (1 - 2 * lax.rem(i, 2)))

            def start():
                pltpu.make_async_remote_copy(
                    src_ref=src.at[m], dst_ref=dst.at[me],
                    send_sem=sem_s, recv_sem=sem_r, device_id=(r, m * 4 + h), device_id_type=MESH,
                ).start()

            if only < NQ:
                pl.when(m < only)(start)
            else:
                start()
            return 0

        lax.fori_loop(0, NQ - 1, go, 0)

    def c_wait(src, dst, sem_r, sem_s, n=NQ - 1):
        return pltpu.make_async_remote_copy(
            src_ref=src.at[pl.ds(0, n)], dst_ref=dst.at[pl.ds(0, n)],
            send_sem=sem_s, recv_sem=sem_r, device_id=(r, c_peer(1) * 4 + h), device_id_type=MESH,
        )

    def q_send(buf, sem_r, sem_s):
        def go(k, _):
            o = q_peer(k)
            pltpu.make_async_remote_copy(
                src_ref=buf.at[h], dst_ref=buf.at[h],
                send_sem=sem_s, recv_sem=sem_r, device_id=(r, me * 4 + o), device_id_type=MESH,
            ).start()
            return 0

        lax.fori_loop(1, 4, go, 0)

    def q_wait(buf, sem_r, sem_s):
        return pltpu.make_async_remote_copy(
            src_ref=buf.at[pl.ds(0, 3)], dst_ref=buf.at[pl.ds(0, 3)],
            send_sem=sem_s, recv_sem=sem_r, device_id=(r, me * 4 + q_peer(1)), device_id_type=MESH,
        )

    zero = jnp.zeros((8, FB), jnp.float32)

    target = target_ref[...]
    member = jnp.where(iota((16, FD), 0) == target, 1.0, 0.0)
    parts = [member[:, i * FB : (i + 1) * FB] for i in range(FD // FB)]
    stacked = jnp.concatenate(parts, axis=0).astype(jnp.bfloat16)
    lanes = iota((FB, 2 * FB), 1)
    summing = jnp.where((iota((FB, 2 * FB), 0) < lanes) | (lanes >= FB), 1.0, 0.0).astype(jnp.bfloat16)
    sums = jnp.dot(stacked, summing, preferred_element_type=jnp.float32)
    count = jnp.zeros((16, FB), jnp.float32)
    ranks = []
    for i, part in enumerate(parts):
        prefix = sums[16 * i : 16 * i + 16, :FB] + count
        ranks.append(jnp.sum(part * prefix, axis=0, keepdims=True))
        count = count + sums[16 * i : 16 * i + 16, FB:]
    rank = jnp.concatenate(ranks, axis=1).astype(jnp.int32)
    hi = target * BPS + rank // FB
    oh_lo[...] = jnp.where(iota((FB, FD), 0) == rank % FB, 1.0, 0.0).astype(jnp.bfloat16)

    for c in range(NC):
        x = x_ref[pl.ds(8 * c, 8), :]
        big = x.astype(jnp.bfloat16)
        small = (x - big.astype(jnp.float32)).astype(jnp.bfloat16)
        both = jnp.concatenate([big, small], axis=0)
        for b in range(NBLK):
            keep = jnp.where(hi == b, 1.0, 0.0).astype(jnp.bfloat16)
            masked[pl.ds(16 * b, 16), :] = both * keep
        placed = lax.dot_general(
            masked[...], oh_lo[...], (((1,), (1,)), ((), ())), preferred_element_type=jnp.float32
        ).reshape(NBLK, 16, FB)
        zout[c][pl.ds(0, NBLK)] = placed[:, :8] + placed[:, 8:]
        zout[c][NBLK] = zero
        if c == 0:
            pl.semaphore_wait(barrier, (NR - 1) + (NQ - 1) + 3)
        z_send(zout[c], zin[c], sr_z.at[c], ss.at[12 + c])
        zin[c][pl.ds(r * BPS, BPS)] = zout[c][pl.ds(r * BPS, BPS)]
        if c == 0:
            blocks = (count.astype(jnp.int32) + (FB - 1)) // FB
            below = jnp.where(iota((16, 16), 1) < iota((16, 16), 0), 1.0, 0.0).astype(jnp.bfloat16)
            start = jnp.dot(
                below, blocks.astype(jnp.float32).astype(jnp.bfloat16), preferred_element_type=jnp.float32
            )
            base = [jnp.sum(part * start, axis=0, keepdims=True) for part in parts]
            hip_ref[...] = jnp.concatenate(base, axis=1).astype(jnp.int32) + rank // FB
            rows = pair_rows(pairs_ref[0:1, :], pairs_ref[1:2, :], owner_ref[...])
            rows = rows + block_rows(start.astype(jnp.int32), blocks)
            bounds = [NBLK - 1, NT - 1, 1, NT, NG - 1, NBLK, NT - 1]
            rows = [jnp.clip(row, 0, high) for row, high in zip(rows, bounds)]
            tabv[...] = jnp.concatenate(rows + [jnp.zeros((1, FB), jnp.int32)], axis=0)
            tab_copy = pltpu.make_async_copy(tabv, tab, tab_sem)
            tab_copy.start()
    tab_copy.wait()

    for t in range(PACKED):
        for c in range(NC):
            gdo[t // 2, t % 2, c] = zout[c][tab[T_IDX, t]]
    c_send(gdo, gdi, sr_gd, ss.at[1], only=ND)
    mdi[NQ - 1, 1] = zero

    def block_of(ref, u):
        return ref[:, u].reshape(NQ * NC * 8, FB)

    def gram(a, b):
        return lax.dot_general(a, b, (((0,), (0,)), ((), ())), precision=HIGHEST, preferred_element_type=jnp.float32)

    for c in range(NC):
        if c == NC - 1:


            @pl.when(handler)
            def _():
                gdi[me] = gdo[me]
                c_wait(gdo, gdi, sr_gd, ss.at[1]).wait_recv()
                for u in range(2):
                    xu = block_of(gdi, u)
                    qd[h, u] = gram(xu, xu)
                q_send(qd, sr_qd, ss.at[2])

        z_wait(zout[c], zin[c], sr_z.at[c], ss.at[12 + c]).wait_recv()
        for k in range(NQ):
            for u in range(2):
                goo[c][k, u] = zin[c][tab[T_UNIT, u * NQ + k]]
        c_send(goo[c], goi[c], sr_go.at[c], ss.at[15 + c])
        goi[c][me] = goo[c][me]

    @pl.when(handler)
    def _():
        q_wait(qd, sr_qd, ss.at[2]).wait_recv()
        eye = jnp.where(iota((FB, FB), 0) == iota((FB, FB), 1), 1.0, 0.0)
        for u in range(2):
            m = qd[0, u] + qd[1, u] + qd[2, u] + qd[3, u]
            mdo[:, u] = m.reshape(NQ, 8, FB)
            shift = m * (1.0 / COEFFICIENT_SIZE) - eye
            change = jnp.dot(block_of(gdi, u), shift, precision=HIGHEST, preferred_element_type=jnp.float32)
            rdo[:, u] = change.reshape(NQ, NC, 8, FB)
        c_send(mdo, mdi, sr_md, ss.at[4])
        mdi[me] = mdo[me]

    total = None
    for c in range(NC):
        c_wait(goo[c], goi[c], sr_go.at[c], ss.at[15 + c]).wait_recv()
        part = gram(goi[c][:, 0].reshape(NQ * 8, FB), goi[c][:, 1].reshape(NQ * 8, FB))
        total = part if total is None else total + part
    qo[h] = total
    q_send(qo, sr_qo, ss.at[5])

    other_handlers(lambda n: c_wait(mdo, mdi, sr_md, ss.at[4], n).wait_recv())
    for d in range(NR):
        t = tab[T_INV, d * BPS + h]
        mzo[d] = mdi[lax.div(t, 2), lax.rem(t, 2)]
    z_send(mzo, mq.at[h], sr_mz, ss.at[6], 1)
    mq[h, r] = mzo[r]

    q_wait(qo, sr_qo, ss.at[5]).wait_recv()
    m = qo[0] + qo[1] + qo[2] + qo[3]
    mko[...] = m.reshape(NQ, 8, FB)
    m = m * (1.0 / COEFFICIENT_SIZE)
    for c in range(NC):
        lc, rc = goi[c][:, 0].reshape(NQ * 8, FB), goi[c][:, 1].reshape(NQ * 8, FB)
        to_left = lax.dot_general(
            rc, m, (((1,), (1,)), ((), ())), precision=HIGHEST, preferred_element_type=jnp.float32
        )
        roo[c][:, 0] = to_left.reshape(NQ, 8, FB)
        roo[c][:, 1] = jnp.dot(lc, m, precision=HIGHEST, preferred_element_type=jnp.float32).reshape(NQ, 8, FB)
        c_send(roo[c], roi[c], sr_ro.at[c], ss.at[18 + c])
        roi[c][me] = roo[c][me]

    c_send(mko, moi, sr_mo, ss.at[8])
    moi[me] = mko[me]

    @pl.when(handler)
    def _():
        c_send(rdo, rdi, sr_rd, ss.at[9])
        rdi[me] = rdo[me]

    seg[NT] = zero
    for c in range(NC):
        c_wait(roo[c], roi[c], sr_ro.at[c], ss.at[18 + c]).wait_recv()
        total = zero
        for i in range(NT):
            p = tab[T_PERM, i]
            total = roi[c][lax.rem(p, NQ), lax.div(p, NQ)] + total * tab[T_SAME, i].astype(jnp.float32)
            seg[i] = total
        for b in range(NBLK):
            zro[c][b] = seg[tab[T_LAST, b]]
        z_send(zro[c], zri[c], sr_zr.at[c], ss.at[21 + c])
        if c == 0:
            z_wait(mzo, mq.at[h], sr_mz, ss.at[6], 1).wait_recv()
            q_send(mq, sr_mq, ss.at[0])
        zri[c][pl.ds(r * BPS, BPS)] = zro[c][pl.ds(r * BPS, BPS)]
        zri[c][NBLK] = zero

    c_wait(mko, moi, sr_mo, ss.at[8]).wait_recv()
    q_wait(mq, sr_mq, ss.at[0]).wait_recv()
    for b in range(NBLK):
        mall[b] = mq[b % BPS, b // BPS]
    mall[pl.ds(NBLK, NQ)] = moi[...]
    for i in range(NQ):
        mfo[i] = mall[tab[T_POS, 4 * i + h]]
    c_send(mfo, mfi, sr_mf, ss.at[11])
    mfi[me] = mfo[me]

    other_handlers(lambda n: c_wait(rdo, rdi, sr_rd, ss.at[9], n).wait_recv())
    hip = hip_ref[...]
    for c in range(NC):
        z_wait(zro[c], zri[c], sr_zr.at[c], ss.at[21 + c]).wait_recv()
        for t in range(PACKED):
            u = gdo[t // 2, t % 2, c] - 0.5 * (rdi[t // 2, t % 2, c] + zri[c][tab[T_IDX, t]])
            big = u.astype(jnp.bfloat16)
            small = (u - big.astype(jnp.float32)).astype(jnp.bfloat16)
            upd[pl.ds(16 * t, 16), :] = jnp.concatenate([big, small], axis=0)
        picked[...] = jnp.dot(upd[...], oh_lo[...], preferred_element_type=jnp.float32)
        total = jnp.zeros((8, FD), jnp.float32)
        for t in range(PACKED):
            both = picked[pl.ds(16 * t, 8), :] + picked[pl.ds(16 * t + 8, 8), :]
            total = total + jnp.where(hip == t, both, 0.0)
        out_ref[pl.ds(8 * c, 8), :] = total

    c_wait(mfo, mfi, sr_mf, ss.at[11]).wait_recv()
    margin_ref[...] = mfi[...].reshape(FB, FB)

    for c in range(NC):
        z_wait(zout[c], zin[c], sr_z.at[c], ss.at[12 + c]).wait_send()
        c_wait(goo[c], goi[c], sr_go.at[c], ss.at[15 + c]).wait_send()
        c_wait(roo[c], roi[c], sr_ro.at[c], ss.at[18 + c]).wait_send()
        z_wait(zro[c], zri[c], sr_zr.at[c], ss.at[21 + c]).wait_send()
    other_handlers(lambda n: c_wait(gdo, gdi, sr_gd, ss.at[1], n).wait_send())

    @pl.when(handler)
    def _():
        q_wait(qd, sr_qd, ss.at[2]).wait_send()
        c_wait(mdo, mdi, sr_md, ss.at[4]).wait_send()
        c_wait(rdo, rdi, sr_rd, ss.at[9]).wait_send()

    q_wait(qo, sr_qo, ss.at[5]).wait_send()
    z_wait(mzo, mq.at[h], sr_mz, ss.at[6], 1).wait_send()
    c_wait(mko, moi, sr_mo, ss.at[8]).wait_send()
    q_wait(mq, sr_mq, ss.at[0]).wait_send()
    c_wait(mfo, mfi, sr_mf, ss.at[11]).wait_send()


def body(coeffs, region_of, block_pairs, block_owner):
    f32, bf16 = jnp.float32, jnp.bfloat16
    v = pltpu.VMEM
    tile = (8, FB)
    dma = pltpu.SemaphoreType.DMA
    vm = pl.BlockSpec(memory_space=pltpu.VMEM)
    z = [v((NBLK + 1, *tile), f32) for _ in range(NC)]
    pr = [v((NQ, 2, *tile), f32) for _ in range(NC)]
    un = v((NQ, 2, NC, *tile), f32)
    corrected, margin = pl.pallas_call(
        kernel,
        out_shape=(
            jax.ShapeDtypeStruct((ROWS, FD), f32),
            jax.ShapeDtypeStruct((FB, FB), f32),
        ),
        in_specs=[vm, vm, vm, vm],
        out_specs=(vm, vm),
        scratch_shapes=[
            v((8, FB), jnp.int32), pltpu.SMEM((8, FB), jnp.int32), v((1, FD), jnp.int32), dma,
            v((FB, FD), bf16), v((NBLK * 16, FD), bf16), z, z, un, un, pr, pr,
            v((4, 2, FB, FB), f32), v((4, FB, FB), f32), un, un, pr, pr, v((NT + 1, *tile), f32), z, z,
            v((NQ, 2, *tile), f32), v((NQ, 2, *tile), f32), v((NR, *tile), f32), v((4, NR, *tile), f32),
            v((NQ, *tile), f32), v((NQ, *tile), f32), v((NG, *tile), f32), v((NQ, *tile), f32), v((NQ, *tile), f32),
            v((PACKED * 16, FB), bf16), v((PACKED * 16, FD), f32),
            dma((24,)), dma((NC,)), dma, dma((NC,)), dma, dma, dma, dma((NC,)), dma((NC,)), dma, dma, dma, dma, dma,
        ],
        compiler_params=pltpu.CompilerParams(collective_id=0, has_side_effects=True, vmem_limit_bytes=56 * 2**20),
    )(coeffs, region_of.reshape(1, FD), block_pairs[0].T, block_owner)
    return corrected, (margin * (1.0 / COEFFICIENT_SIZE))[None, None]


def solution(mesh):
    placed = (P("group", "region"), P("region", None), P("region", None, None), P("region", None))
    return jax.shard_map(
        body,
        mesh=mesh,
        in_specs=placed,
        out_specs=(P("group", "region"), P("region", "group", None, None)),
        check_vma=False,
    )
```
